128 devices in a mesh: seq: 32 (over z, x, core), bkt: 4 (over y).
Axes of the slice: x: 4, y: 4, z: 4, core: 2. Of those that a mesh axis runs over, the one named last changes fastest.
Arguments:
- tokens: bfloat16 [8192, 4096], P('seq'), may hold values from -6 to 6
- weights: bfloat16 [4096, 2, 2048], P(None, None, 'bkt'), may hold values from -0.09375 to 0.09375
- cotangent: bfloat16 [8192, 2048], P('seq', 'bkt'), may hold values from -6 to 6
- buckets: int32 [2, 16, 8192], P(None, 'bkt', 'seq'), may hold values from 0 to 63, as said below
Outputs:
- token_grads: bfloat16 [8192, 4096], P(('seq', 'bkt'))
The draws below stay inside these ranges and needn't reach their ends.
Inputs may be any that keep to these rules, and one draw needn't show every extreme that they name: In every round and head, the tokens of one seq shard that fall into the buckets b with b // 2 == k number at most 12, and for one k every shard has exactly 12; a bucket holds at most 192 tokens, and some hold exactly 192; every bucket holds tokens of every shard.
All inputs are finite; a program needn't handle non-finite values.
Results may differ from the reference program's by a relative error of at most 0.025.
Values may be sent and summed in bfloat16 or wider, within the bound.
No kernel may reach another device: no remote copies, remote signals or barrier semaphores. Data moves between devices by JAX's collectives and lax.ppermute only.
A program may use at most 128 MiB of HBM per device.

```python
import math
import jax
import jax.numpy as jnp
from jax import lax

D = 4096
HS = 128
HEADS = 16
NB = 64
ROUNDS = 2
TOK_DEV = 256
TOKENS = 8192
BPO = 2
BCAP = 256
N_SEQ = 32


def one_table(key):
    key_pairs, key_owner, key_order, key_shuffle = jax.random.split(key, 4)
    mean_count = TOK_DEV // NB
    reach = mean_count // 2
    pair_count = NB // 2
    spread = jax.random.randint(key_pairs, (N_SEQ, pair_count), 0, reach + 1)
    forced = jnp.arange(pair_count) < BPO
    spread = jnp.where(forced[None, :], reach, spread)
    counts = jnp.stack([mean_count + spread, mean_count - spread], axis=-1).reshape(N_SEQ, NB).astype(jnp.int32)
    labels = jnp.arange(NB, dtype=jnp.int32)
    chosen = jax.random.randint(key_owner, (), 0, N_SEQ)
    scramble = jax.random.permutation(key_order, NB).astype(jnp.int32)
    label_list = jnp.argsort(jnp.where(labels // BPO == chosen, 0, NB) + scramble).astype(jnp.int32)
    heavy_first = jnp.argsort(jnp.where((labels % 2 == 0) & (labels // 2 < BPO), 0, NB) + labels).astype(jnp.int32)
    label_of = label_list[jnp.argsort(heavy_first)]
    device_keys = jax.random.split(key_shuffle, N_SEQ)

    def one_device(device_key, device_counts):
        internal = jnp.repeat(labels, device_counts, total_repeat_length=TOK_DEV)
        return label_of[jax.random.permutation(device_key, internal)]
    return jax.vmap(one_device)(device_keys, counts).reshape(TOKENS)


def draw_buckets(key, part):
    key = jax.random.fold_in(key, 7)
    table_keys = jax.random.split(key, ROUNDS * HEADS)
    return jax.vmap(one_table)(table_keys).reshape(ROUNDS, HEADS, TOKENS).astype(jnp.int32)


def common_part(key):
    key_dirs, key_signs = jax.random.split(key, 2)
    directions = jnp.where(jax.random.bernoulli(key_dirs, 0.5, (4, D)), 1.0, -1.0).astype(jnp.float32)
    signs = jnp.where(jax.random.bernoulli(key_signs, 0.5, (TOKENS, 4)), 1.0, -1.0).astype(jnp.float32)
    total = jnp.zeros((TOKENS, D), jnp.float32)
    for index in range(4):
        total = total + signs[:, index:index + 1] * directions[index][None, :]
    return total


def draw_tokens(key, part):
    key = jax.random.fold_in(key, 11)
    key_common, key_noise = jax.random.split(key, 2)
    noise = jax.random.normal(key_noise, (TOKENS, D), jnp.float32)
    shared = common_part(key_common)
    return jnp.clip(shared + noise, -6.0, 6.0).astype(jnp.bfloat16)


def block_levels(key, dims, shards, smallest, largest):
    def one(axis_at, parts):
        steps = jax.random.uniform(jax.random.fold_in(jax.random.fold_in(key, 6), axis_at), (parts,), jnp.float32, smallest / len(shards), largest / len(shards))
        return jnp.repeat(jnp.exp(steps), dims[axis_at] // parts).reshape((-1,) + (1,) * (len(dims) - axis_at - 1))

    loudness = one(*shards[0])
    for cut in shards[1:]:
        loudness = loudness * one(*cut)
    return loudness


def scatter_about(stream_key, dims, width, bound, shards=(), kind=jnp.bfloat16):
    drawn = width * jax.random.normal(stream_key, dims, jnp.float32)
    if shards:
        drawn = drawn * block_levels(stream_key, dims, shards, -0.22, 0.18)
    return jnp.clip(drawn, -bound, bound).astype(kind)


def setup_inputs(seed: int = 0) -> dict:
    arg_keys = jax.random.split(jax.random.key(seed), 5)
    tokens = draw_tokens(jax.random.fold_in(arg_keys[4], 71), 0)
    weights = scatter_about(arg_keys[1], (D, 2, HEADS * HS), D ** -0.5, 0.09375, ((2, 4),))
    cotangent = scatter_about(arg_keys[2], (TOKENS, HEADS * HS), 1.0, 6.0, ((0, 32), (1, 4)))
    buckets = draw_buckets(jax.random.fold_in(arg_keys[4], 71), 0)
    return dict(tokens=tokens, weights=weights, cotangent=cotangent, buckets=buckets)


SELF_SCORE = -100000.0
FAR_SCORE = -1000000000.0
HIGHEST_PRECISION = lax.Precision.HIGHEST

def attend(query, values, places, present):
    head_size = query.shape[-1]
    unit_keys = (query * lax.rsqrt(lax.optimization_barrier(jnp.sum(query * query, axis=-1, keepdims=True)) + 1e-06)).astype(jnp.bfloat16)
    unit_keys = lax.optimization_barrier(unit_keys).astype(jnp.float32)
    scores = jnp.dot(query, unit_keys.T, precision=HIGHEST_PRECISION) * (1.0 / math.sqrt(head_size))
    row_ids = jnp.arange(query.shape[0], dtype=jnp.int32)
    allowed = present[None, :] & (places[None, :] <= places[:, None])
    scores = jnp.where(allowed, scores, FAR_SCORE)
    scores = jnp.where(row_ids[:, None] == row_ids[None, :], SELF_SCORE, scores)
    row_max = lax.stop_gradient(lax.optimization_barrier(jnp.max(scores, axis=-1, keepdims=True)))
    shifted = jnp.exp(scores - row_max)
    totals = lax.optimization_barrier(jnp.sum(shifted, axis=-1, keepdims=True))
    probs = lax.optimization_barrier((shifted / totals).astype(jnp.bfloat16)).astype(jnp.float32)
    outputs = jnp.dot(probs, values, precision=HIGHEST_PRECISION)
    return (outputs, row_max[:, 0] + jnp.log(totals[:, 0]))

def attend_blocks(query, values, places, present):
    block_rows = query.shape[-2]
    head_size = query.shape[-1]
    outputs, lse = jax.vmap(attend)(query.reshape(-1, block_rows, head_size), values.reshape(-1, block_rows, head_size), places.reshape(-1, block_rows), present.reshape(-1, block_rows))
    return (outputs.reshape(query.shape), lse.reshape(places.shape))

def block_grads(query, values, places, present, out_grad, lse_grad):

    def forward(query_rows, value_rows):
        return attend_blocks(query_rows, value_rows, places, present)
    _, pull = jax.vjp(forward, query, values)
    return pull((out_grad, lse_grad))

def bucket_plan(keys, group_count, group_size, capacity):
    row_count = keys.shape[0]
    ordering = jnp.argsort(keys, stable=True).astype(jnp.int32)
    targets = (keys // group_size).astype(jnp.int32)
    matches = (targets[:, None] == jnp.arange(group_count, dtype=jnp.int32)[None, :]).astype(jnp.int32)
    counts = lax.optimization_barrier(jnp.sum(matches, axis=0)).astype(jnp.int32)
    starts = (jnp.cumsum(counts) - counts).astype(jnp.int32)
    slot_ids = jnp.arange(capacity, dtype=jnp.int32)
    filled = slot_ids[None, :] < counts[:, None]
    sources = ordering[jnp.clip(starts[:, None] + slot_ids[None, :], 0, row_count - 1)]
    inverse = jnp.argsort(ordering).astype(jnp.int32)
    returns = targets * capacity + inverse - starts[jnp.clip(targets, 0, group_count - 1)]
    return (sources, filled, returns)

def pick_rows(source_rows, sources, filled):
    picked = source_rows[sources]
    keep_mask = filled.reshape(filled.shape + (1,) * (picked.ndim - filled.ndim))
    return jnp.where(keep_mask, picked, jnp.zeros((), picked.dtype))

def put_back(flattened, positions):
    return flattened[jnp.clip(positions, 0, flattened.shape[0] - 1)]

def round_cotangents(round_out, round_lse, cotangent, round_count):
    item_count, row_count, head_size = round_out.shape
    head_count = item_count // round_count
    round_values = round_out.astype(jnp.float32).reshape(round_count, head_count, row_count, head_size)
    round_logs = round_lse.reshape(round_count, head_count, row_count)
    round_share = jax.nn.softmax(round_logs, axis=0)
    upstream = cotangent.reshape(row_count, head_count, head_size).transpose(1, 0, 2).astype(jnp.float32)
    inner = lax.optimization_barrier(jnp.sum(upstream[None] * round_values, axis=-1))
    lse_grad = round_share * (inner - lax.optimization_barrier(jnp.sum(round_share * inner, axis=0)))
    out_grad = (round_share[..., None] * upstream[None]).astype(jnp.bfloat16)
    return (out_grad.reshape(item_count, row_count, head_size), lse_grad.reshape(item_count, row_count))

def sum_rounds(per_round, round_count):
    item_count, row_count, head_size = per_round.shape
    head_count = item_count // round_count
    summed = per_round.astype(jnp.float32).reshape(round_count, head_count, row_count, head_size).sum(axis=0)
    return summed.astype(jnp.bfloat16).transpose(1, 0, 2).reshape(row_count, head_count * head_size)

def reference(tokens, weights, cotangent, buckets):
    flat_weights = weights.reshape(D, 2 * HEADS * HS).astype(jnp.float32)
    projected = jnp.dot(tokens.astype(jnp.float32), flat_weights, precision=HIGHEST_PRECISION)
    projected = projected.reshape(TOKENS, 2, HEADS * HS).astype(jnp.bfloat16)
    shared = projected[:, 0].reshape(TOKENS, HEADS, HS).transpose(1, 0, 2)
    values = projected[:, 1].reshape(TOKENS, HEADS, HS).transpose(1, 0, 2)
    row_ids = buckets.reshape(ROUNDS * HEADS, TOKENS)
    head_ids = jnp.tile(jnp.arange(HEADS, dtype=jnp.int32), ROUNDS)

    def arrange(bucket_row, head_index):
        sources, present, returns = bucket_plan(bucket_row, NB, 1, BCAP)
        query_lay = pick_rows(shared[head_index], sources, present).astype(jnp.float32)
        value_lay = pick_rows(values[head_index], sources, present).astype(jnp.float32)
        place_lay = jnp.where(present, sources, -1).astype(jnp.int32)
        return (query_lay, value_lay, place_lay, present, sources, returns)

    def forward_item(pair):
        bucket_row, head_index = pair
        query_lay, value_lay, place_lay, present, sources, returns = arrange(bucket_row, head_index)
        outputs, lse = attend_blocks(query_lay, value_lay, place_lay, present)
        return (put_back(outputs.astype(jnp.bfloat16).reshape(-1, HS), returns), put_back(lse.reshape(-1), returns))
    round_out, round_lse = lax.map(forward_item, (row_ids, head_ids))
    out_grad, lse_grad = round_cotangents(round_out, round_lse, cotangent, ROUNDS)

    def backward_item(group):
        bucket_row, head_index, grad_rows, lse_rows = group
        query_lay, value_lay, place_lay, present, sources, returns = arrange(bucket_row, head_index)
        grad_lay = pick_rows(grad_rows, sources, present).astype(jnp.float32)
        lse_lay = pick_rows(lse_rows, sources, present)
        query_grad, value_grad = block_grads(query_lay, value_lay, place_lay, present, grad_lay, lse_lay)
        return (put_back(query_grad.astype(jnp.bfloat16).reshape(-1, HS), returns), put_back(value_grad.astype(jnp.bfloat16).reshape(-1, HS), returns))
    query_each, value_each = lax.map(backward_item, (row_ids, head_ids, out_grad, lse_grad))
    grads = jnp.stack([sum_rounds(query_each, ROUNDS), sum_rounds(value_each, ROUNDS)], axis=1)
    token_grads = jnp.dot(grads.reshape(TOKENS, 2 * HEADS * HS).astype(jnp.float32), flat_weights.T, precision=HIGHEST_PRECISION)
    return token_grads.astype(jnp.bfloat16)
```

```python
import functools
import math

import jax
import jax.numpy as jnp
from jax import lax
from jax.experimental import pallas as pl
from jax.experimental.pallas import tpu as pltpu
from jax.sharding import PartitionSpec as P

HH = 4
RR = 2
TT = 256
HS = 128
NO = 32
CAP = 12
ROWS = NO * 24
SLOTS = NO * CAP
MAIN = NO * 8
ITEMS = HH * RR
SCALE = 1.0 / math.sqrt(HS)
SELF_SCORE = -100000.0
FAR = -(2.0**30)
F32 = jnp.float32
BF = jnp.bfloat16
VMEM = 40 * 1024 * 1024


def iota(shape, axis):
    return lax.broadcasted_iota(jnp.int32, shape, axis)


def dot(a, b, ca=1, cb=0, precision=None):
    return lax.dot_general(
        a, b, (((ca,), (cb,)), ((), ())), preferred_element_type=F32, precision=precision
    )


def halves(x):
    high = x.astype(BF)
    return high, (x - high.astype(F32)).astype(BF)


def slots_kernel(odd_ref, buckets_ref, rows_ref):
    odd = odd_ref[0]
    owners = lax.shift_right_logical(buckets_ref[...], 1)
    before = (iota((TT, TT), 0) < iota((TT, TT), 1)).astype(BF)
    for item in range(ITEMS):
        mine = owners[item : item + 1, :]
        hot = iota((NO, TT), 0) == mine
        counts = dot(hot.astype(BF), before)
        rank = jnp.sum(jnp.where(hot, counts, 0.0), axis=0, keepdims=True).astype(jnp.int32)
        first = item // HH
        late = 4 * odd if first == 0 else 4 - 4 * odd
        row = jnp.where(rank < 8, rank + 16 * first, rank + late)
        rows_ref[item : item + 1, :] = mine * 24 + row


def slot_rows(odd, buckets):
    return pl.pallas_call(
        slots_kernel,
        out_shape=jax.ShapeDtypeStruct((ITEMS, TT), jnp.int32),
        in_specs=[
            pl.BlockSpec(memory_space=pltpu.SMEM),
            pl.BlockSpec(memory_space=pltpu.VMEM),
        ],
        out_specs=pl.BlockSpec(memory_space=pltpu.VMEM),
        name="slots",
    )(odd, buckets)


WIRE = HH * 3 * HS + 128


def dispatch_kernel(rows_ref, buckets_ref, proj_ref, cot_ref, out_ref):
    row_ids = iota((ROWS, TT), 0)
    marks = jnp.zeros((ROWS, 128), F32)
    for h in range(HH):
        first = row_ids == rows_ref[h : h + 1, :]
        second = row_ids == rows_ref[HH + h : HH + h + 1, :]
        code0 = (1 + (buckets_ref[h : h + 1, :] & 1)).astype(F32)
        code1 = (1 + (buckets_ref[HH + h : HH + h + 1, :] & 1)).astype(F32)
        code = jnp.where(first, code0, jnp.where(second, code1, 0.0)).astype(BF)
        hot = (first | second).astype(BF)
        lanes = pl.ds(h * HS, HS)
        source = jnp.concatenate(
            [proj_ref[0, :, lanes], proj_ref[1, :, lanes], cot_ref[:, lanes]], axis=1
        )
        out_ref[:, pl.ds(h * 3 * HS, 3 * HS)] = dot(hot, source).astype(BF)
        marks += dot(code, (iota((TT, 128), 1) == h).astype(BF))
    out_ref[:, pl.ds(HH * 3 * HS, 128)] = marks.astype(BF)


def dispatch(rows, buckets, proj, cot):
    return pl.pallas_call(
        dispatch_kernel,
        out_shape=jax.ShapeDtypeStruct((ROWS, WIRE), BF),
        compiler_params=pltpu.CompilerParams(vmem_limit_bytes=VMEM),
        name="dispatch",
    )(rows, buckets, proj, cot)


def split_rounds(x):
    width = x.shape[1]
    x = x.reshape(NO, 3, 8, width)
    mixed = x[:, 1].reshape(NO // 2, 2, 8, width)
    even, odd = mixed[:, 0], mixed[:, 1]
    top = iota((NO // 2, 8, width), 1) < 4
    late0 = jnp.where(top, even, odd).reshape(SLOTS - MAIN, width)
    late1 = jnp.where(top, odd, even).reshape(SLOTS - MAIN, width)
    return (
        jnp.concatenate([x[:, 0].reshape(MAIN, width), late0], axis=0),
        jnp.concatenate([x[:, 2].reshape(MAIN, width), late1], axis=0),
    )


def join_rounds(x0, x1):
    width = x0.shape[1]
    late0 = x0[MAIN:].reshape(NO // 2, 8, width)
    late1 = x1[MAIN:].reshape(NO // 2, 8, width)
    top = iota((NO // 2, 8, width), 1) < 4
    even = jnp.where(top, late0, late1)
    odd = jnp.where(top, late1, late0)
    mixed = jnp.stack([even, odd], axis=1).reshape(NO, 1, 8, width)
    main0 = x0[:MAIN].reshape(NO, 1, 8, width)
    main1 = x1[:MAIN].reshape(NO, 1, 8, width)
    return jnp.concatenate([main0, mixed, main1], axis=1).reshape(ROWS, width)


def source_and_slot(shape, axis, which):
    row = iota(shape, axis)
    late = row - MAIN
    flip = ((late & 7) >= 4).astype(jnp.int32)
    source_late = 2 * lax.shift_right_arithmetic(late, 3) + (flip if which == 0 else 1 - flip)
    source = jnp.where(row < MAIN, lax.shift_right_logical(row, 3), source_late)
    slot = jnp.where(row < MAIN, row & 7, 8 + (late & 3))
    return source, slot


def forward_kernel(x_ref, marks_ref, probs_ref, rows_ref, self_ref, wire_ref, bias, spread):
    h = pl.program_id(0)

    @pl.when(h == 0)
    def _():
        for r in range(RR):
            source_i, slot_i = source_and_slot((SLOTS, SLOTS), 0, r)
            source_j, slot_j = source_and_slot((SLOTS, SLOTS), 1, r)
            earlier = source_j * CAP + slot_j < source_i * CAP + slot_i
            bias[r] = jnp.where(earlier, 0.0, FAR)
        spread[...] = jnp.zeros_like(spread)

    rounds = split_rounds(x_ref[...].astype(F32))
    marks = split_rounds(marks_ref[...].astype(F32))
    lane = iota((SLOTS, HS), 1)
    for r in range(RR):
        x = rounds[r].astype(BF)
        q = rounds[r][:, :HS]
        u = rounds[r][:, 2 * HS :]
        v_half = x[:, HS : 2 * HS]
        code = jnp.sum(jnp.where(lane == h, marks[r], 0.0), axis=1, keepdims=True)
        scale = lax.rsqrt(jnp.sum(q * q, axis=1, keepdims=True) + 1e-06)
        unit = (q * scale).astype(BF)
        in1 = (code == 1.0).astype(F32)
        in2 = (code == 2.0).astype(F32)
        far_q = jnp.where(lane == 0, FAR * in1, jnp.where(lane == 1, FAR * in2, 0.0))
        far_q = jnp.where(lane == 2, FAR * (1.0 - in1 - in2), far_q).astype(BF)
        far_k = jnp.where(lane == 0, 1.0 - in1, jnp.where(lane == 1, 1.0 - in2, 0.0))
        far_k = jnp.where(lane == 2, 1.0, far_k).astype(BF)
        scores = dot(
            jnp.concatenate([x[:, :HS], far_q], axis=1),
            jnp.concatenate([unit, far_k], axis=1),
            1,
            1,
        )
        scores = scores * SCALE + bias[r]
        top = jnp.maximum(jnp.max(scores, axis=1, keepdims=True), SELF_SCORE)
        shifted = jnp.exp(scores - top)
        own = jnp.exp(SELF_SCORE - top)
        totals = jnp.sum(shifted, axis=1, keepdims=True) + own
        inverse = 1.0 / totals
        probs = (shifted * inverse).astype(BF)
        own = (own * inverse).astype(BF).astype(F32)
        out = dot(probs, v_half) + own * rounds[r][:, HS : 2 * HS]
        out = out.astype(BF).astype(F32)
        inner = jnp.sum(u * out, axis=1, keepdims=True)
        lse = top + jnp.log(totals)
        probs_ref[0, r] = probs
        rows_ref[0, r] = x
        self_ref[0, r] = jnp.where(
            lane == 0, own, jnp.where(lane == 1, inner, jnp.where(lane == 2, scale, 0.0))
        )
        _, slot = source_and_slot((SLOTS, HS), 0, r)
        here = lane == slot + (r * HH + h) * CAP
        spread[r, :, :HS] += jnp.where(here, lse, 0.0)
        spread[r, :, HS:] += jnp.where(here, inner, 0.0)

    @pl.when(h == HH - 1)
    def _():
        total = jnp.zeros((NO, 2 * HS), F32)
        for r in range(RR):
            source, _ = source_and_slot((NO, SLOTS), 1, r)
            hot = (source == iota((NO, SLOTS), 0)).astype(F32)
            total += dot(hot, spread[r], precision=lax.Precision.HIGHEST)
        wire_ref[:, 0, :] = total[:, :HS]
        wire_ref[:, 1, :] = total[:, HS:]


def forward(received):
    return pl.pallas_call(
        forward_kernel,
        grid=(HH,),
        out_shape=(
            jax.ShapeDtypeStruct((HH, RR, SLOTS, SLOTS), BF),
            jax.ShapeDtypeStruct((HH, RR, SLOTS, 3 * HS), BF),
            jax.ShapeDtypeStruct((HH, RR, SLOTS, HS), F32),
            jax.ShapeDtypeStruct((NO, 2, HS), F32),
        ),
        in_specs=[
            pl.BlockSpec((ROWS, 3 * HS), lambda h: (0, h)),
            pl.BlockSpec((ROWS, 128), lambda h: (0, HH * 3)),
        ],
        out_specs=(
            pl.BlockSpec((1, RR, SLOTS, SLOTS), lambda h: (h, 0, 0, 0)),
            pl.BlockSpec((1, RR, SLOTS, 3 * HS), lambda h: (h, 0, 0, 0)),
            pl.BlockSpec((1, RR, SLOTS, HS), lambda h: (h, 0, 0, 0)),
            pl.BlockSpec((NO, 2, HS), lambda h: (0, 0, 0)),
        ),
        scratch_shapes=[
            pltpu.VMEM((RR, SLOTS, SLOTS), F32),
            pltpu.VMEM((RR, SLOTS, 2 * HS), F32),
        ],
        compiler_params=pltpu.CompilerParams(vmem_limit_bytes=VMEM),
        name="forward",
    )(received, received)


def between_kernel(probs_ref, rows_ref, self_ref, weighted_ref, first_ref, second_ref):
    for r in range(RR):
        probs = probs_ref[0, r]
        q = rows_ref[0, r, :, :HS]
        v = rows_ref[0, r, :, HS : 2 * HS]
        u = rows_ref[0, r, :, 2 * HS :]
        inner = self_ref[0, r, :, 1:2]
        scale = self_ref[0, r, :, 2:3]
        unit = (q.astype(F32) * scale).astype(BF)
        weighted = (probs.astype(F32) * (dot(u, v, 1, 1) - inner)).astype(BF)
        weighted_ref[0, r] = weighted
        first_ref[0, r] = dot(weighted, unit)
        second_ref[0, r] = dot(probs, unit)


def between(probs, rows, own):
    square = pl.BlockSpec((1, RR, SLOTS, SLOTS), lambda h: (h, 0, 0, 0))
    narrow = pl.BlockSpec((1, RR, SLOTS, HS), lambda h: (h, 0, 0, 0))
    wide = pl.BlockSpec((1, RR, SLOTS, 3 * HS), lambda h: (h, 0, 0, 0))
    flops = ITEMS * SLOTS * SLOTS * HS * 6
    return pl.pallas_call(
        between_kernel,
        grid=(HH,),
        out_shape=(
            jax.ShapeDtypeStruct((HH, RR, SLOTS, SLOTS), BF),
            jax.ShapeDtypeStruct((HH, RR, SLOTS, HS), F32),
            jax.ShapeDtypeStruct((HH, RR, SLOTS, HS), F32),
        ),
        in_specs=[square, wide, narrow],
        out_specs=(square, narrow, narrow),
        compiler_params=pltpu.CompilerParams(vmem_limit_bytes=VMEM),
        cost_estimate=pl.CostEstimate(flops=flops, bytes_accessed=12 << 20, transcendentals=0),
        name="between",
    )(probs, rows, own)


def shares_kernel(buckets_ref, got_ref, out_ref):
    got = jnp.concatenate([got_ref[:, 0, :], got_ref[:, 1, :]], axis=1)
    got_high, got_low = halves(got)
    got2 = jnp.concatenate([got_high, got_low], axis=0)
    owners = lax.shift_right_logical(buckets_ref[...], 1)
    before = (iota((TT, TT), 1) < iota((TT, TT), 0)).astype(BF)
    lane = iota((TT, HS), 1)
    total = jnp.zeros((NO, 2 * HS), F32)
    for h in range(HH):
        logs, inners, heres, hots = [], [], [], []
        for r in range(RR):
            item = r * HH + h
            hot = iota((TT, NO), 1) == owners[:, item : item + 1]
            counts = dot(before, hot.astype(BF))
            rank = jnp.sum(jnp.where(hot, counts, 0.0), axis=1, keepdims=True).astype(jnp.int32)
            hot = hot.astype(BF)
            seen = dot(jnp.concatenate([hot, hot], axis=1), got2)
            here = lane == rank + item * CAP
            logs.append(jnp.sum(jnp.where(here, seen[:, :HS], 0.0), axis=1, keepdims=True))
            inners.append(jnp.sum(jnp.where(here, seen[:, HS:], 0.0), axis=1, keepdims=True))
            heres.append(here)
            hots.append(hot)
        top = jnp.maximum(logs[0], logs[1])
        weights = [jnp.exp(logs[0] - top), jnp.exp(logs[1] - top)]
        inverse = 1.0 / (weights[0] + weights[1])
        share = [weights[0] * inverse, weights[1] * inverse]
        gap = inners[1] - inners[0]
        shift = [share[1] * gap, -share[0] * gap]
        for r in range(RR):
            back = jnp.concatenate(
                [jnp.where(heres[r], share[r], 0.0), jnp.where(heres[r], shift[r], 0.0)], axis=1
            )
            high, low = halves(back)
            total += dot(hots[r], high, 0, 0) + dot(hots[r], low, 0, 0)
    out_ref[:, 0, :] = total[:, :HS]
    out_ref[:, 1, :] = total[:, HS:]


def shares(buckets, got):
    return pl.pallas_call(
        shares_kernel,
        out_shape=jax.ShapeDtypeStruct((NO, 2, HS), F32),
        compiler_params=pltpu.CompilerParams(vmem_limit_bytes=VMEM),
        name="shares",
    )(buckets, got)


def backward_kernel(
    probs_ref, weighted_ref, rows_ref, self_ref, first_ref, second_ref, back_ref, out_ref
):
    h = pl.program_id(0)
    back = jnp.concatenate([back_ref[:, 0, :], back_ref[:, 1, :]], axis=1)
    high, low = halves(back)
    back2 = jnp.concatenate([high, low], axis=0)
    lane = iota((SLOTS, HS), 1)
    grads = []
    for r in range(RR):
        source, _ = source_and_slot((SLOTS, NO), 0, r)
        hot = (source == iota((SLOTS, NO), 1)).astype(BF)
        seen = dot(jnp.concatenate([hot, hot], axis=1), back2)
        _, slot = source_and_slot((SLOTS, HS), 0, r)
        here = lane == slot + (r * HH + h) * CAP
        share = jnp.sum(jnp.where(here, seen[:, :HS], 0.0), axis=1, keepdims=True)
        shift = jnp.sum(jnp.where(here, seen[:, HS:], 0.0), axis=1, keepdims=True)
        probs = probs_ref[0, r]
        weighted = weighted_ref[0, r]
        q = rows_ref[0, r, :, :HS].astype(F32)
        u = rows_ref[0, r, :, 2 * HS :].astype(F32)
        own = self_ref[0, r, :, 0:1]
        scale = self_ref[0, r, :, 2:3]
        q_share = share * q
        u_share = share * u
        right = jnp.concatenate([-shift * q_share, u_share], axis=1).astype(BF)
        both = dot(probs, right, 0, 0)
        unit_grad = (dot(weighted, q_share.astype(BF), 0, 0) + both[:, :HS]) * SCALE
        value_grad = both[:, HS:] + own * u_share
        along = jnp.sum(q * unit_grad, axis=1, keepdims=True)
        query_grad = share * (first_ref[0, r] - shift * second_ref[0, r]) * SCALE
        query_grad += scale * unit_grad - q * (scale * scale * scale * along)
        grads.append(jnp.concatenate([query_grad, value_grad], axis=1))
    out_ref[...] = join_rounds(grads[0], grads[1]).astype(BF)


def backward(probs, weighted, rows, own, first, second, back):
    square = pl.BlockSpec((1, RR, SLOTS, SLOTS), lambda h: (h, 0, 0, 0))
    narrow = pl.BlockSpec((1, RR, SLOTS, HS), lambda h: (h, 0, 0, 0))
    wide = pl.BlockSpec((1, RR, SLOTS, 3 * HS), lambda h: (h, 0, 0, 0))
    return pl.pallas_call(
        backward_kernel,
        grid=(HH,),
        out_shape=jax.ShapeDtypeStruct((ROWS, HH * 2 * HS), BF),
        in_specs=[
            square,
            square,
            wide,
            narrow,
            narrow,
            narrow,
            pl.BlockSpec((NO, 2, HS), lambda h: (0, 0, 0)),
        ],
        out_specs=pl.BlockSpec((ROWS, 2 * HS), lambda h: (0, h)),
        compiler_params=pltpu.CompilerParams(vmem_limit_bytes=VMEM),
        name="backward",
    )(probs, weighted, rows, own, first, second, back)


def collect_kernel(rows_ref, got_ref, out_ref):
    row_ids = iota((ROWS, TT), 0)
    for h in range(HH):
        first = row_ids == rows_ref[h : h + 1, :]
        second = row_ids == rows_ref[HH + h : HH + h + 1, :]
        hot = (first | second).astype(BF)
        sums = dot(hot, got_ref[:, pl.ds(h * 2 * HS, 2 * HS)], 0, 0).astype(BF)
        out_ref[0, :, pl.ds(h * HS, HS)] = sums[:, :HS]
        out_ref[1, :, pl.ds(h * HS, HS)] = sums[:, HS:]


def collect(rows, got):
    return pl.pallas_call(
        collect_kernel,
        out_shape=jax.ShapeDtypeStruct((2, TT, HH * HS), BF),
        compiler_params=pltpu.CompilerParams(vmem_limit_bytes=VMEM),
        name="collect",
    )(rows, got)


def exchange(x):
    return lax.all_to_all(x, "seq", split_axis=0, concat_axis=0, tiled=True)


def per_device(tokens, weights, cotangent, buckets):
    flat = buckets.reshape(ITEMS, TT)
    odd = (lax.axis_index("seq") % 2).astype(jnp.int32).reshape(1)
    rows = slot_rows(odd, flat)
    projected = jnp.einsum(
        "td,dcf->ctf", tokens, weights, preferred_element_type=jnp.float32
    ).astype(jnp.bfloat16)
    received = exchange(dispatch(rows, flat, projected, cotangent))
    probs, held, own, wire = forward(received)
    home = exchange(wire)
    weighted, first, second = between(probs, held, own)
    back = exchange(shares(flat.T, home))
    slot_grads = exchange(backward(probs, weighted, held, own, first, second, back))
    grads = collect(rows, slot_grads)
    return lax.psum_scatter(
        jnp.einsum("ctf,dcf->td", grads, weights, preferred_element_type=jnp.float32).astype(
            jnp.bfloat16
        ),
        "bkt",
        scatter_dimension=0,
        tiled=True,
    )


def solution(mesh):
    in_specs = (P("seq", None), P(None, None, "bkt"), P("seq", "bkt"), P(None, "bkt", "seq"))
    out_specs = P(("seq", "bkt"), None)
    return jax.shard_map(
        per_device, mesh=mesh, in_specs=in_specs, out_specs=out_specs, check_vma=False
    )
```

```python
import functools
import math

import jax
import jax.numpy as jnp
from jax import lax
from jax.experimental import pallas as pl
from jax.experimental.pallas import tpu as pltpu
from jax.sharding import PartitionSpec as P

HH = 4
RR = 2
TT = 256
HS = 128
NO = 32
CAP = 12
ROWS = NO * 24
SLOTS = NO * CAP
MAIN = NO * 8
ITEMS = HH * RR
SCALE = 1.0 / math.sqrt(HS)
POWER = SCALE / math.log(2.0)
SELF_SCORE = -100000.0
FAR = -(2.0**30)
F32 = jnp.float32
BF = jnp.bfloat16
VMEM = 24 * 1024 * 1024


def iota(shape, axis):
    return lax.broadcasted_iota(jnp.int32, shape, axis)


def dot(a, b, ca=1, cb=0, precision=None):
    return lax.dot_general(
        a, b, (((ca,), (cb,)), ((), ())), preferred_element_type=F32, precision=precision
    )


def halves(x):
    high = x.astype(BF)
    return high, (x - high.astype(F32)).astype(BF)


WIRE = HH * 3 * HS + 128


def dispatch_kernel(odd_ref, buckets_ref, proj_ref, cot_ref, rows_ref, out_ref):
    odd = odd_ref[0]
    before = (iota((TT, TT), 0) < iota((TT, TT), 1)).astype(BF)
    owner_ids = iota((NO, TT), 0)
    row_ids = iota((ROWS, TT), 0)
    buckets = [buckets_ref[r, h : h + 1, :] for r in range(RR) for h in range(HH)]
    hots = [owner_ids == lax.shift_right_logical(mine, 1) for mine in buckets]
    counts = dot(jnp.concatenate([hot.astype(BF) for hot in hots], axis=0), before)
    rows = []
    for item in range(ITEMS):
        count = counts[item * NO : (item + 1) * NO]
        rank = jnp.sum(jnp.where(hots[item], count, 0.0), axis=0, keepdims=True)
        rank = rank.astype(jnp.int32)
        first = item // HH
        late = 4 * odd if first == 0 else 4 - 4 * odd
        row = jnp.where(rank < 8, rank + 16 * first, rank + late)
        rows.append(lax.shift_right_logical(buckets[item], 1) * 24 + row)
        rows_ref[item : item + 1, :] = rows[item]
    marks = jnp.zeros((ROWS, 128), F32)
    for h in range(HH):
        first = row_ids == rows[h]
        second = row_ids == rows[HH + h]
        code0 = (1 + (buckets[h] & 1)).astype(F32)
        code1 = (1 + (buckets[HH + h] & 1)).astype(F32)
        code = jnp.where(first, code0, jnp.where(second, code1, 0.0)).astype(BF)
        hot = (first | second).astype(BF)
        lanes = pl.ds(h * HS, HS)
        source = jnp.concatenate(
            [proj_ref[0, :, lanes], proj_ref[1, :, lanes], cot_ref[:, lanes]], axis=1
        )
        out_ref[:, pl.ds(h * 3 * HS, 3 * HS)] = dot(hot, source).astype(BF)
        marks += dot(code, (iota((TT, 128), 1) == h).astype(BF))
    out_ref[:, pl.ds(HH * 3 * HS, 128)] = marks.astype(BF)


def dispatch(odd, buckets, proj, cot):
    vmem = pl.BlockSpec(memory_space=pltpu.VMEM)
    return pl.pallas_call(
        dispatch_kernel,
        out_shape=(
            jax.ShapeDtypeStruct((ITEMS, TT), jnp.int32),
            jax.ShapeDtypeStruct((ROWS, WIRE), BF),
        ),
        in_specs=[pl.BlockSpec(memory_space=pltpu.SMEM), vmem, vmem, vmem],
        compiler_params=pltpu.CompilerParams(vmem_limit_bytes=VMEM),
        name="dispatch",
    )(odd, buckets, proj, cot)


def split_rounds(x):
    width = x.shape[1]
    x = x.reshape(NO, 3, 8, width)
    mixed = x[:, 1].reshape(NO // 2, 2, 8, width)
    even, odd = mixed[:, 0], mixed[:, 1]
    top = iota((NO // 2, 8, width), 1) < 4
    late0 = jnp.where(top, even, odd).reshape(SLOTS - MAIN, width)
    late1 = jnp.where(top, odd, even).reshape(SLOTS - MAIN, width)
    return (
        jnp.concatenate([x[:, 0].reshape(MAIN, width), late0], axis=0),
        jnp.concatenate([x[:, 2].reshape(MAIN, width), late1], axis=0),
    )


def join_rounds(x0, x1):
    width = x0.shape[1]
    late0 = x0[MAIN:].reshape(NO // 2, 8, width)
    late1 = x1[MAIN:].reshape(NO // 2, 8, width)
    top = iota((NO // 2, 8, width), 1) < 4
    even = jnp.where(top, late0, late1)
    odd = jnp.where(top, late1, late0)
    mixed = jnp.stack([even, odd], axis=1).reshape(NO, 1, 8, width)
    main0 = x0[:MAIN].reshape(NO, 1, 8, width)
    main1 = x1[:MAIN].reshape(NO, 1, 8, width)
    return jnp.concatenate([main0, mixed, main1], axis=1).reshape(ROWS, width)


def source_and_slot(shape, axis, which):
    row = iota(shape, axis)
    late = row - MAIN
    flip = ((late & 7) >= 4).astype(jnp.int32)
    source_late = 2 * lax.shift_right_arithmetic(late, 3) + (flip if which == 0 else 1 - flip)
    source = jnp.where(row < MAIN, lax.shift_right_logical(row, 3), source_late)
    slot = jnp.where(row < MAIN, row & 7, 8 + (late & 3))
    return source, slot


def forward_kernel(x_ref, marks_ref, probs_ref, rows_ref, self_ref, wire_ref, bias, spread):
    h = pl.program_id(0)

    @pl.when(h == 0)
    def _():
        for r in range(RR):
            source_i, slot_i = source_and_slot((SLOTS, 1), 0, r)
            source_j, slot_j = source_and_slot((1, SLOTS), 1, r)
            earlier = source_j * CAP + slot_j < source_i * CAP + slot_i
            bias[r] = jnp.where(earlier, 0.0, FAR)
        spread[...] = jnp.zeros_like(spread)

    rounds = split_rounds(x_ref[...].astype(F32))
    marks = split_rounds(marks_ref[...].astype(F32))
    lane = iota((SLOTS, HS), 1)
    for r in range(RR):
        x = rounds[r].astype(BF)
        q = rounds[r][:, :HS]
        u = rounds[r][:, 2 * HS :]
        v_half = x[:, HS : 2 * HS]
        code = jnp.sum(jnp.where(lane == h, marks[r], 0.0), axis=1, keepdims=True)
        scale = lax.rsqrt(jnp.sum(q * q, axis=1, keepdims=True) + 1e-06)
        unit = (q * scale).astype(BF)
        in1 = (code == 1.0).astype(F32)
        in2 = (code == 2.0).astype(F32)
        far_q = jnp.where(lane == 0, FAR * in1, jnp.where(lane == 1, FAR * in2, 0.0))
        far_q = jnp.where(lane == 2, FAR * (1.0 - in1 - in2), far_q).astype(BF)
        far_k = jnp.where(lane == 0, 1.0 - in1, jnp.where(lane == 1, 1.0 - in2, 0.0))
        far_k = jnp.where(lane == 2, 1.0, far_k).astype(BF)
        scores = dot(
            jnp.concatenate([x[:, :HS], far_q], axis=1),
            jnp.concatenate([unit, far_k], axis=1),
            1,
            1,
        )
        scores = scores + bias[r]
        top = jnp.maximum(jnp.max(scores, axis=1, keepdims=True), SELF_SCORE / SCALE)
        shifted = jnp.exp2(scores * POWER - top * POWER)
        own = jnp.exp2((SELF_SCORE / SCALE) * POWER - top * POWER)
        totals = jnp.sum(shifted, axis=1, keepdims=True) + own
        inverse = 1.0 / totals
        probs = (shifted * inverse).astype(BF)
        own = (own * inverse).astype(BF).astype(F32)
        out = dot(probs, v_half) + own * rounds[r][:, HS : 2 * HS]
        out = out.astype(BF).astype(F32)
        inner = jnp.sum(u * out, axis=1, keepdims=True)
        lse = top * SCALE + jnp.log(totals)
        probs_ref[0, r] = probs
        rows_ref[0, r] = x
        self_ref[0, r] = jnp.where(
            lane == 0, own, jnp.where(lane == 1, inner, jnp.where(lane == 2, scale, 0.0))
        )
        _, slot = source_and_slot((SLOTS, HS), 0, r)
        here = lane == slot + (r * HH + h) * CAP
        spread[r, :, :HS] += jnp.where(here, lse, 0.0)
        spread[r, :, HS:] += jnp.where(here, inner, 0.0)

    @pl.when(h == HH - 1)
    def _():
        total = jnp.zeros((NO, 2 * HS), F32)
        for r in range(RR):
            source, _ = source_and_slot((NO, SLOTS), 1, r)
            hot = (source == iota((NO, SLOTS), 0)).astype(BF)
            high, low = halves(spread[r])
            total += dot(hot, high) + dot(hot, low)
        wire_ref[:, 0, :] = total[:, :HS]
        wire_ref[:, 1, :] = total[:, HS:]


def forward(received):
    return pl.pallas_call(
        forward_kernel,
        grid=(HH,),
        out_shape=(
            pltpu.HBM((HH, RR, SLOTS, SLOTS), BF),
            pltpu.HBM((HH, RR, SLOTS, 3 * HS), BF),
            pltpu.HBM((HH, RR, SLOTS, HS), F32),
            jax.ShapeDtypeStruct((NO, 2, HS), F32),
        ),
        in_specs=[
            pl.BlockSpec((ROWS, 3 * HS), lambda h: (0, h)),
            pl.BlockSpec((ROWS, 128), lambda h: (0, 3 * HH)),
        ],
        out_specs=(
            pl.BlockSpec((1, RR, SLOTS, SLOTS), lambda h: (h, 0, 0, 0)),
            pl.BlockSpec((1, RR, SLOTS, 3 * HS), lambda h: (h, 0, 0, 0)),
            pl.BlockSpec((1, RR, SLOTS, HS), lambda h: (h, 0, 0, 0)),
            pl.BlockSpec((NO, 2, HS), lambda h: (0, 0, 0)),
        ),
        scratch_shapes=[
            pltpu.VMEM((RR, SLOTS, SLOTS), F32),
            pltpu.VMEM((RR, SLOTS, 2 * HS), F32),
        ],
        compiler_params=pltpu.CompilerParams(vmem_limit_bytes=VMEM),
        name="forward",
    )(received, received)


def between_kernel(probs_ref, rows_ref, self_ref, probs_t_ref, weighted_t_ref, sums_ref):
    for r in range(RR):
        probs = probs_ref[0, r]
        q = rows_ref[0, r, :, :HS]
        v = rows_ref[0, r, :, HS : 2 * HS]
        u = rows_ref[0, r, :, 2 * HS :]
        own = self_ref[0, r, :, 0:1]
        inner = self_ref[0, r, :, 1:2]
        scale = self_ref[0, r, :, 2:3]
        unit = (q.astype(F32) * scale).astype(BF)
        weighted = (probs.astype(F32) * (dot(u, v, 1, 1) - inner)).astype(BF)
        probs_t_ref[0, r] = probs.T
        weighted_t_ref[0, r] = weighted.T
        sums_ref[0, r, :, :HS] = dot(weighted, unit).astype(BF)
        sums_ref[0, r, :, HS : 2 * HS] = dot(probs, unit).astype(BF)
        sums_ref[0, r, :, 2 * HS :] = jnp.broadcast_to(own, (SLOTS, HS)).astype(BF)


SQUARE = pl.BlockSpec((1, RR, SLOTS, SLOTS), lambda h: (h, 0, 0, 0))
NARROW = pl.BlockSpec((1, RR, SLOTS, HS), lambda h: (h, 0, 0, 0))
WIDE = pl.BlockSpec((1, RR, SLOTS, 3 * HS), lambda h: (h, 0, 0, 0))


def between(probs, rows, own):
    flops = ITEMS * SLOTS * SLOTS * HS * 6
    return pl.pallas_call(
        between_kernel,
        grid=(HH,),
        out_shape=(
            pltpu.HBM((HH, RR, SLOTS, SLOTS), BF),
            pltpu.HBM((HH, RR, SLOTS, SLOTS), BF),
            pltpu.HBM((HH, RR, SLOTS, 3 * HS), BF),
        ),
        in_specs=[SQUARE, WIDE, NARROW],
        out_specs=(SQUARE, SQUARE, WIDE),
        compiler_params=pltpu.CompilerParams(vmem_limit_bytes=VMEM),
        cost_estimate=pl.CostEstimate(flops=flops, bytes_accessed=12 << 20, transcendentals=0),
        name="between",
    )(pinned(probs), pinned(rows), pinned(own))


def ranks_kernel(buckets_ref, out_ref):
    owners = lax.shift_right_logical(buckets_ref[...], 1)
    before = (iota((TT, TT), 1) < iota((TT, TT), 0)).astype(BF)
    hots = [iota((TT, NO), 1) == owners[:, item : item + 1] for item in range(ITEMS)]
    counts = dot(before, jnp.concatenate([hot.astype(BF) for hot in hots], axis=1))
    for item in range(ITEMS):
        count = counts[:, item * NO : (item + 1) * NO]
        rank = jnp.sum(jnp.where(hots[item], count, 0.0), axis=1, keepdims=True)
        out_ref[:, item : item + 1] = rank.astype(jnp.int32) + item * CAP


def ranks(buckets):
    return pl.pallas_call(
        ranks_kernel,
        out_shape=jax.ShapeDtypeStruct((TT, ITEMS), jnp.int32),
        compiler_params=pltpu.CompilerParams(vmem_limit_bytes=VMEM),
        name="ranks",
    )(buckets)


def shares_kernel(buckets_ref, columns_ref, ranks_ref, got_ref, out_ref):
    got = jnp.concatenate([got_ref[:, 0, :], got_ref[:, 1, :]], axis=1)
    got_high, got_low = halves(got)
    got2 = jnp.concatenate([got_high, got_low], axis=0)
    lane = iota((TT, HS), 1)
    lane2 = iota((TT, 2 * NO), 1) & (NO - 1)
    total = jnp.zeros((NO, 2 * HS), F32)
    for h in range(HH):
        logs, inners, heres = [], [], []
        for r in range(RR):
            item = r * HH + h
            owner = lax.shift_right_logical(columns_ref[:, item : item + 1], 1)
            seen = dot((lane2 == owner).astype(BF), got2)
            here = lane == ranks_ref[:, item : item + 1]
            logs.append(jnp.sum(jnp.where(here, seen[:, :HS], 0.0), axis=1, keepdims=True))
            inners.append(jnp.sum(jnp.where(here, seen[:, HS:], 0.0), axis=1, keepdims=True))
            heres.append(here)
        top = jnp.maximum(logs[0], logs[1])
        weights = [jnp.exp(logs[0] - top), jnp.exp(logs[1] - top)]
        inverse = 1.0 / (weights[0] + weights[1])
        share = [weights[0] * inverse, weights[1] * inverse]
        gap = inners[1] - inners[0]
        shift = [share[1] * gap, -share[0] * gap]
        for r in range(RR):
            owner = lax.shift_right_logical(buckets_ref[r, h : h + 1, :], 1)
            hot = (iota((NO, TT), 0) == owner).astype(BF)
            back = jnp.concatenate(
                [jnp.where(heres[r], share[r], 0.0), jnp.where(heres[r], shift[r], 0.0)], axis=1
            )
            high, low = halves(back)
            total += dot(
                jnp.concatenate([hot, hot], axis=1), jnp.concatenate([high, low], axis=0)
            )
    out_ref[:, 0, :] = total[:, :HS]
    out_ref[:, 1, :] = total[:, HS:]


def shares(buckets, columns, rank_columns, got):
    return pl.pallas_call(
        shares_kernel,
        out_shape=jax.ShapeDtypeStruct((NO, 2, HS), F32),
        compiler_params=pltpu.CompilerParams(vmem_limit_bytes=VMEM),
        name="shares",
    )(buckets, columns, rank_columns, got)


def backward_kernel(probs_ref, weighted_ref, q_ref, u_ref, sums_ref, back_ref, out_ref, seen):
    h = pl.program_id(0)

    @pl.when(h == 0)
    def _():
        back = jnp.concatenate([back_ref[:, 0, :], back_ref[:, 1, :]], axis=1)
        high, low = halves(back)
        back2 = jnp.concatenate([high, low], axis=0)
        lane2 = iota((SLOTS, 2 * NO), 1) & (NO - 1)
        for r in range(RR):
            source, _ = source_and_slot((SLOTS, 1), 0, r)
            seen[r] = dot((source == lane2).astype(BF), back2)

    lane = iota((SLOTS, HS), 1)
    grads = []
    for r in range(RR):
        _, slot = source_and_slot((SLOTS, 1), 0, r)
        here = lane == slot + (r * HH + h) * CAP
        share = jnp.sum(jnp.where(here, seen[r, :, :HS], 0.0), axis=1, keepdims=True)
        shift = jnp.sum(jnp.where(here, seen[r, :, HS:], 0.0), axis=1, keepdims=True)
        q = q_ref[0, r].astype(F32)
        u_share = share * u_ref[0, r].astype(F32)
        q_share = share * q
        right = jnp.concatenate([-shift * q_share, u_share], axis=1).astype(BF)
        both = dot(probs_ref[0, r], right)
        unit_grad = (dot(weighted_ref[0, r], q_share.astype(BF)) + both[:, :HS]) * SCALE
        value_grad = both[:, HS:] + sums_ref[0, r, :, 2 * HS :].astype(F32) * u_share
        scale = lax.rsqrt(jnp.sum(q * q, axis=1, keepdims=True) + 1e-06)
        along = jnp.sum(q * unit_grad, axis=1, keepdims=True)
        first = sums_ref[0, r, :, :HS].astype(F32)
        second = sums_ref[0, r, :, HS : 2 * HS].astype(F32)
        query_grad = (share * SCALE) * (first - shift * second)
        query_grad += scale * unit_grad - q * (scale * scale * scale * along)
        grads.append(jnp.concatenate([query_grad, value_grad], axis=1))
    out_ref[...] = join_rounds(grads[0], grads[1]).astype(BF)


def pinned(x):
    return pltpu.with_memory_space_constraint(x, pltpu.HBM)


def backward(probs, weighted, rows, sums, back):
    return pl.pallas_call(
        backward_kernel,
        grid=(HH,),
        out_shape=jax.ShapeDtypeStruct((ROWS, HH * 2 * HS), BF),
        in_specs=[
            SQUARE,
            SQUARE,
            pl.BlockSpec((1, RR, SLOTS, HS), lambda h: (h, 0, 0, 0)),
            pl.BlockSpec((1, RR, SLOTS, HS), lambda h: (h, 0, 0, 2)),
            WIDE,
            pl.BlockSpec((NO, 2, HS), lambda h: (0, 0, 0)),
        ],
        out_specs=pl.BlockSpec((ROWS, 2 * HS), lambda h: (0, h)),
        scratch_shapes=[pltpu.VMEM((RR, SLOTS, 2 * HS), F32)],
        compiler_params=pltpu.CompilerParams(vmem_limit_bytes=VMEM),
        name="backward",
    )(pinned(probs), pinned(weighted), pinned(rows), pinned(rows), pinned(sums), back)


def collect_kernel(rows_ref, got_ref, out_ref):
    row_ids = iota((ROWS, TT), 0)
    for h in range(HH):
        first = row_ids == rows_ref[h : h + 1, :]
        second = row_ids == rows_ref[HH + h : HH + h + 1, :]
        hot = (first | second).astype(BF)
        sums = dot(hot, got_ref[:, pl.ds(h * 2 * HS, 2 * HS)], 0, 0).astype(BF)
        out_ref[0, :, pl.ds(h * HS, HS)] = sums[:, :HS]
        out_ref[1, :, pl.ds(h * HS, HS)] = sums[:, HS:]


def collect(rows, got):
    return pl.pallas_call(
        collect_kernel,
        out_shape=jax.ShapeDtypeStruct((2, TT, HH * HS), BF),
        compiler_params=pltpu.CompilerParams(vmem_limit_bytes=VMEM),
        name="collect",
    )(rows, got)


def exchange(x):
    return lax.all_to_all(x, "seq", split_axis=0, concat_axis=0, tiled=True)


def block_order(me):
    return [me, me ^ 3, me ^ 1, me ^ 2]


def blocks_of(x, me):
    size = x.shape[1] // 4
    parts = [lax.dynamic_slice_in_dim(x, i * size, size, 1) for i in block_order(me)]
    return jnp.concatenate(parts, axis=1)


def swap(x, mask):
    return lax.ppermute(x, "bkt", [(i, i ^ mask) for i in range(4)])


def per_device(tokens, weights, cotangent, buckets):
    odd = (lax.axis_index("seq") & 1).astype(jnp.int32).reshape(1)
    me = lax.axis_index("bkt")
    projected = jnp.einsum(
        "td,dcf->ctf", tokens, weights, preferred_element_type=jnp.float32
    ).astype(jnp.bfloat16)
    rows, send = dispatch(odd, buckets, projected, cotangent)
    received = exchange(send)
    columns = buckets.reshape(ITEMS, TT).T
    rank_columns = ranks(columns)
    rows = blocks_of(rows, me)
    probs, held, own, wire = forward(received)
    home = exchange(wire)
    probs_t, weighted_t, sums = between(probs, held, own)
    back = exchange(shares(buckets, columns, rank_columns, home))
    slot_grads = exchange(backward(probs_t, weighted_t, held, sums, back))
    grads = collect(rows, slot_grads)
    half = weights.shape[0] // 2
    one, two = (
        jnp.einsum("ctf,dcf->td", grads, w, preferred_element_type=jnp.float32)
        .astype(jnp.bfloat16)
        .reshape(4, TT // 4, half)
        for w in (weights[:half], weights[half:])
    )
    got_one = swap(one[2:], 1)
    got_two = swap(jnp.stack([two[1], two[3]]), 3)
    sum_one = one[:2] + got_one
    sum_two = jnp.stack([two[0], two[2]]) + got_two
    out_one = sum_one[0] + swap(sum_one[1], 3)
    out_two = sum_two[0] + swap(sum_two[1], 1)
    return jnp.concatenate([out_one, out_two], axis=1)


def solution(mesh):
    in_specs = (P("seq", None), P(None, None, "bkt"), P("seq", "bkt"), P(None, "bkt", "seq"))
    out_specs = P(("seq", "bkt"), None)
    return jax.shard_map(
        per_device, mesh=mesh, in_specs=in_specs, out_specs=out_specs, check_vma=False
    )
```

```python
import functools
import math

import jax
import jax.numpy as jnp
from jax import lax
from jax.experimental import pallas as pl
from jax.experimental.pallas import tpu as pltpu
from jax.sharding import PartitionSpec as P

HH = 4
RR = 2
TT = 256
HS = 128
NO = 32
CAP = 12
ROWS = NO * 24
SLOTS = NO * CAP
MAIN = NO * 8
ITEMS = HH * RR
SCALE = 1.0 / math.sqrt(HS)
POWER = SCALE / math.log(2.0)
SELF_SCORE = -100000.0
FAR = -(2.0**30)
F32 = jnp.float32
BF = jnp.bfloat16
VMEM = 24 * 1024 * 1024


def iota(shape, axis):
    return lax.broadcasted_iota(jnp.int32, shape, axis)


def dot(a, b, ca=1, cb=0, precision=None):
    return lax.dot_general(
        a, b, (((ca,), (cb,)), ((), ())), preferred_element_type=F32, precision=precision
    )


def halves(x):
    high = x.astype(BF)
    return high, (x - high.astype(F32)).astype(BF)


WIRE = HH * 3 * HS + 128
OWNERS = 32
PLACES = 40
CODES = 64


def dispatch_kernel(odd_ref, buckets_ref, proj_ref, cot_ref, rows_ref, out_ref):
    odd = odd_ref[0]
    before = (iota((TT, TT), 0) < iota((TT, TT), 1)).astype(BF)
    owner_ids = iota((NO, TT), 0)
    row_ids = iota((ROWS, TT), 0)
    buckets = [buckets_ref[r, h : h + 1, :] for r in range(RR) for h in range(HH)]
    hots = [owner_ids == lax.shift_right_logical(mine, 1) for mine in buckets]
    counts = dot(jnp.concatenate([hot.astype(BF) for hot in hots], axis=0), before)
    rows, ranks = [], []
    for item in range(ITEMS):
        count = counts[item * NO : (item + 1) * NO]
        rank = jnp.sum(jnp.where(hots[item], count, 0.0), axis=0, keepdims=True)
        rank = rank.astype(jnp.int32)
        first = item // HH
        late = 4 * odd if first == 0 else 4 - 4 * odd
        row = jnp.where(rank < 8, rank + 16 * first, rank + late)
        rows.append(lax.shift_right_logical(buckets[item], 1) * 24 + row)
        ranks.append(rank)
        rows_ref[item : item + 1, :] = rows[item]
    code_ids = iota((128, TT), 0)
    marks = jnp.zeros((ROWS, 128), F32)
    for h in range(HH):
        first = (row_ids == rows[h]).astype(BF)
        second = (row_ids == rows[HH + h]).astype(BF)
        hot = first + second
        codes = []
        for item, other in ((h, HH + h), (HH + h, h)):
            code = jnp.where((code_ids >= CODES) & (code_ids & 7 == h), 1 + (buckets[item] & 1), 0)
            owner = lax.shift_right_logical(buckets[other], 1)
            code = jnp.where(code_ids == OWNERS + item, owner, code)
            codes.append(jnp.where(code_ids == PLACES + item, ranks[other], code))
        codes = jnp.concatenate(codes, axis=1).astype(F32).astype(BF)
        lanes = pl.ds(h * HS, HS)
        source = jnp.concatenate(
            [proj_ref[0, :, lanes], proj_ref[1, :, lanes], cot_ref[:, lanes]], axis=1
        )
        out_ref[:, pl.ds(h * 3 * HS, 3 * HS)] = dot(hot, source).astype(BF)
        marks += dot(jnp.concatenate([first, second], axis=1), codes, 1, 1)
    out_ref[:, pl.ds(HH * 3 * HS, 128)] = marks.astype(BF)


def dispatch(odd, buckets, proj, cot):
    vmem = pl.BlockSpec(memory_space=pltpu.VMEM)
    return pl.pallas_call(
        dispatch_kernel,
        out_shape=(
            jax.ShapeDtypeStruct((ITEMS, TT), jnp.int32),
            jax.ShapeDtypeStruct((ROWS, WIRE), BF),
        ),
        in_specs=[pl.BlockSpec(memory_space=pltpu.SMEM), vmem, vmem, vmem],
        compiler_params=pltpu.CompilerParams(vmem_limit_bytes=VMEM),
        name="dispatch",
    )(odd, buckets, proj, cot)


def split_rounds(x):
    width = x.shape[1]
    x = x.reshape(NO, 3, 8, width)
    mixed = x[:, 1].reshape(NO // 2, 2, 8, width)
    even, odd = mixed[:, 0], mixed[:, 1]
    top = iota((NO // 2, 8, width), 1) < 4
    late0 = jnp.where(top, even, odd).reshape(SLOTS - MAIN, width)
    late1 = jnp.where(top, odd, even).reshape(SLOTS - MAIN, width)
    return (
        jnp.concatenate([x[:, 0].reshape(MAIN, width), late0], axis=0),
        jnp.concatenate([x[:, 2].reshape(MAIN, width), late1], axis=0),
    )


def join_rounds(x0, x1):
    width = x0.shape[1]
    late0 = x0[MAIN:].reshape(NO // 2, 8, width)
    late1 = x1[MAIN:].reshape(NO // 2, 8, width)
    top = iota((NO // 2, 8, width), 1) < 4
    even = jnp.where(top, late0, late1)
    odd = jnp.where(top, late1, late0)
    mixed = jnp.stack([even, odd], axis=1).reshape(NO, 1, 8, width)
    main0 = x0[:MAIN].reshape(NO, 1, 8, width)
    main1 = x1[:MAIN].reshape(NO, 1, 8, width)
    return jnp.concatenate([main0, mixed, main1], axis=1).reshape(ROWS, width)


def source_and_slot(shape, axis, which):
    row = iota(shape, axis)
    late = row - MAIN
    flip = ((late & 7) >= 4).astype(jnp.int32)
    source_late = 2 * lax.shift_right_arithmetic(late, 3) + (flip if which == 0 else 1 - flip)
    source = jnp.where(row < MAIN, lax.shift_right_logical(row, 3), source_late)
    slot = jnp.where(row < MAIN, row & 7, 8 + (late & 3))
    return source, slot


def forward_kernel(
    x_ref, marks_ref, probs_ref, rows_ref, self_ref, wire_ref, mine_ref, bias, spread, far
):
    h = pl.program_id(0)
    lane = iota((SLOTS, HS), 1)

    @pl.when(h == 0)
    def _():
        for r in range(RR):
            source_i, slot_i = source_and_slot((SLOTS, 1), 0, r)
            source_j, slot_j = source_and_slot((1, SLOTS), 1, r)
            earlier = source_j * CAP + slot_j < source_i * CAP + slot_i
            bias[r] = jnp.where(earlier, 0.0, FAR)
        for r, marks in enumerate(split_rounds(marks_ref[...].astype(F32))):
            spread[r] = jnp.where((lane >= OWNERS) & (lane < CODES), marks, 0.0)
            group = lane & (HS - 8)
            wanted = jnp.where(group == CODES, 1.0, jnp.where(group == CODES + 8, 2.0, 0.0))
            coded = (group >= CODES) & (group < CODES + 24)
            far[r, :, :HS] = jnp.where(coded & (marks == wanted), FAR, 0.0).astype(BF)
            other = coded & ((marks != wanted) | (group == CODES + 16))
            far[r, :, HS:] = jnp.where(other, 1.0, 0.0).astype(BF)

    rounds = split_rounds(x_ref[...].astype(F32))
    head = ((lane & 7) == h).astype(BF)
    for r in range(RR):
        x = rounds[r].astype(BF)
        q = rounds[r][:, :HS]
        u = rounds[r][:, 2 * HS :]
        v_half = x[:, HS : 2 * HS]
        scale = lax.rsqrt(jnp.sum(q * q, axis=1, keepdims=True) + 1e-06)
        unit = (q * scale).astype(BF)
        far_q = far[r, :, :HS] * head
        far_k = far[r, :, HS:]
        scores = dot(
            jnp.concatenate([x[:, :HS], far_q], axis=1),
            jnp.concatenate([unit, far_k], axis=1),
            1,
            1,
        )
        scores = scores + bias[r]
        top = jnp.maximum(jnp.max(scores, axis=1, keepdims=True), SELF_SCORE / SCALE)
        shifted = jnp.exp2(scores * POWER - top * POWER)
        own = jnp.exp2((SELF_SCORE / SCALE) * POWER - top * POWER)
        totals = jnp.sum(shifted, axis=1, keepdims=True) + own
        inverse = 1.0 / totals
        probs = (shifted * inverse).astype(BF)
        own = (own * inverse).astype(BF).astype(F32)
        out = dot(probs, v_half) + own * rounds[r][:, HS : 2 * HS]
        out = out.astype(BF).astype(F32)
        inner = jnp.sum(u * out, axis=1, keepdims=True)
        lse = top * SCALE + jnp.log(totals)
        probs_ref[0, r] = probs
        rows_ref[0, r] = x
        kept = 0.0
        for at, column in enumerate((own, inner, scale)):
            kept = jnp.where(lane == at, column.astype(F32), kept)
        self_ref[0, r] = kept
        high, low = halves(lse)
        sent = 0.0
        for at, column in enumerate((high, low, inner.astype(BF))):
            sent = jnp.where(lane == (r * HH + h) * 3 + at, column.astype(F32), sent)
        spread[r] += sent

    @pl.when(h == HH - 1)
    def _():
        total = jnp.zeros((HS, SLOTS), F32)
        for r in range(RR):
            source, slot = source_and_slot((SLOTS, 1), 0, r)
            hot = (iota((SLOTS, SLOTS), 1) == slot * NO + source).astype(BF)
            total += dot(spread[r].astype(BF), hot, 0, 0)
        total = total.astype(BF)
        mine_ref[...] = total
        total = total[: 3 * ITEMS]
        for k in range(NO):
            wire_ref[pl.ds(k * 3 * ITEMS, 3 * ITEMS), :] = total


def forward(received):
    return pl.pallas_call(
        forward_kernel,
        grid=(HH,),
        out_shape=(
            pltpu.HBM((HH, RR, SLOTS, SLOTS), BF),
            pltpu.HBM((HH, RR, SLOTS, 3 * HS), BF),
            pltpu.HBM((HH, RR, SLOTS, HS), F32),
            jax.ShapeDtypeStruct((NO * 3 * ITEMS, SLOTS), BF),
            pltpu.HBM((HS, SLOTS), BF),
        ),
        in_specs=[
            pl.BlockSpec((ROWS, 3 * HS), lambda h: (0, h)),
            pl.BlockSpec((ROWS, 128), lambda h: (0, 3 * HH)),
        ],
        out_specs=(
            pl.BlockSpec((1, RR, SLOTS, SLOTS), lambda h: (h, 0, 0, 0)),
            pl.BlockSpec((1, RR, SLOTS, 3 * HS), lambda h: (h, 0, 0, 0)),
            pl.BlockSpec((1, RR, SLOTS, HS), lambda h: (h, 0, 0, 0)),
            pl.BlockSpec((NO * 3 * ITEMS, SLOTS), lambda h: (0, 0)),
            pl.BlockSpec((HS, SLOTS), lambda h: (0, 0)),
        ),
        scratch_shapes=[
            pltpu.VMEM((RR, SLOTS, SLOTS), F32),
            pltpu.VMEM((RR, SLOTS, HS), F32),
            pltpu.VMEM((RR, SLOTS, 2 * HS), BF),
        ],
        compiler_params=pltpu.CompilerParams(vmem_limit_bytes=VMEM),
        name="forward",
    )(received, received)


def between_kernel(probs_ref, rows_ref, self_ref, probs_t_ref, weighted_t_ref, sums_ref):
    for r in range(RR):
        probs = probs_ref[0, r]
        q = rows_ref[0, r, :, :HS]
        v = rows_ref[0, r, :, HS : 2 * HS]
        u = rows_ref[0, r, :, 2 * HS :]
        inner = self_ref[0, r, :, 1:2]
        scale = self_ref[0, r, :, 2:3]
        unit = (q.astype(F32) * scale).astype(BF)
        weighted = (probs.astype(F32) * (dot(u, v, 1, 1) - inner)).astype(BF)
        probs_t_ref[0, r] = probs.T
        weighted_t_ref[0, r] = weighted.T
        sums_ref[0, r, :, :HS] = dot(weighted, unit).astype(BF)
        sums_ref[0, r, :, HS : 2 * HS] = dot(probs, unit).astype(BF)
        own = self_ref[0, r, :, 0:1]
        sums_ref[0, r, :, 2 * HS :] = jnp.broadcast_to(own, (SLOTS, HS)).astype(BF)


SQUARE = pl.BlockSpec((1, RR, SLOTS, SLOTS), lambda h: (h, 0, 0, 0))
NARROW = pl.BlockSpec((1, RR, SLOTS, HS), lambda h: (h, 0, 0, 0))
WIDE = pl.BlockSpec((1, RR, SLOTS, 3 * HS), lambda h: (h, 0, 0, 0))


def between(probs, rows, own):
    flops = ITEMS * SLOTS * SLOTS * HS * 6
    return pl.pallas_call(
        between_kernel,
        grid=(HH,),
        out_shape=(
            pltpu.HBM((HH, RR, SLOTS, SLOTS), BF),
            pltpu.HBM((HH, RR, SLOTS, SLOTS), BF),
            pltpu.HBM((HH, RR, SLOTS, 3 * HS), BF),
        ),
        in_specs=[SQUARE, WIDE, NARROW],
        out_specs=(SQUARE, SQUARE, WIDE),
        compiler_params=pltpu.CompilerParams(vmem_limit_bytes=VMEM),
        cost_estimate=pl.CostEstimate(flops=flops, bytes_accessed=12 << 20, transcendentals=0),
        name="between",
    )(pinned(probs), pinned(rows), pinned(own))


def round_shares(mine_ref, got_ref, got, put):
    for at in range(SLOTS // HS):
        got[at] = got_ref[:, pl.ds(at * HS, HS)].astype(F32)
    mine = mine_ref[...].astype(F32)
    owner_ids = iota((NO, SLOTS), 0).astype(F32)
    slot_ids = iota((SLOTS, SLOTS), 0)
    source = iota((1, SLOTS), 1) & (NO - 1)
    mine_lse, mine_inner, other_lse, other_inner = [], [], [], []
    for item in range(ITEMS):
        first_row = (item ^ HH) * 3
        high, low, inners = (
            jnp.concatenate(
                [
                    got[i, pl.ds(first_row + at, NO, stride=3 * ITEMS), :]
                    for i in range(SLOTS // HS)
                ],
                axis=1,
            ).astype(BF)
            for at in range(3)
        )
        hot = (owner_ids == mine[OWNERS + item : OWNERS + item + 1]).astype(BF)
        place = mine[PLACES + item : PLACES + item + 1].astype(jnp.int32) * NO + source
        here = slot_ids == place
        table = jnp.concatenate([high, low], axis=0)
        logs = dot(table, jnp.concatenate([hot, hot], axis=0), 0, 0)
        inners = dot(inners, hot, 0, 0)
        other_lse.append(jnp.sum(jnp.where(here, logs, 0.0), axis=0, keepdims=True))
        other_inner.append(jnp.sum(jnp.where(here, inners, 0.0), axis=0, keepdims=True))
        mine_lse.append(mine[item * 3 : item * 3 + 1] + mine[item * 3 + 1 : item * 3 + 2])
        mine_inner.append(mine[item * 3 + 2 : item * 3 + 3])
    mine_lse, mine_inner, other_lse, other_inner = (
        jnp.concatenate(x, axis=0) for x in (mine_lse, mine_inner, other_lse, other_inner)
    )
    top = jnp.maximum(mine_lse, other_lse)
    share = jnp.exp(mine_lse - top)
    other_share = jnp.exp(other_lse - top)
    inverse = 1.0 / (share + other_share)
    share = share * inverse
    shift = other_share * inverse * (other_inner - mine_inner)
    high, low = halves(jnp.concatenate([share, shift], axis=0))
    both = jnp.concatenate([high, low], axis=1)
    for r in range(RR):
        source, slot = source_and_slot((SLOTS, 1), 0, r)
        hot = (iota((SLOTS, SLOTS), 1) == slot * NO + source).astype(BF)
        columns = dot(jnp.concatenate([hot, hot], axis=1), both, 1, 1)
        for h in range(HH):
            item = r * HH + h
            put[h, r, :, :HS] = jnp.broadcast_to(columns[:, item : item + 1], (SLOTS, HS))
            item += ITEMS
            put[h, r, :, HS:] = jnp.broadcast_to(columns[:, item : item + 1], (SLOTS, HS))


def backward_kernel(
    probs_ref, weighted_ref, q_ref, u_ref, sums_ref, mine_ref, got_ref, out_ref, got, put
):
    h = pl.program_id(0)

    @pl.when(h == 0)
    def _():
        round_shares(mine_ref, got_ref, got, put)

    grads = []
    for r in range(RR):
        share = put[h, r, :, :HS]
        shift = put[h, r, :, HS:]
        q = q_ref[0, r].astype(F32)
        u_share = share * u_ref[0, r].astype(F32)
        q_share = share * q
        right = jnp.concatenate([-shift * q_share, u_share], axis=1).astype(BF)
        both = dot(probs_ref[0, r], right)
        unit_grad = (dot(weighted_ref[0, r], q_share.astype(BF)) + both[:, :HS]) * SCALE
        value_grad = both[:, HS:] + sums_ref[0, r, :, 2 * HS :].astype(F32) * u_share
        scale = lax.rsqrt(jnp.sum(q * q, axis=1, keepdims=True) + 1e-06)
        along = jnp.sum(q * unit_grad, axis=1, keepdims=True)
        first = sums_ref[0, r, :, :HS].astype(F32)
        second = sums_ref[0, r, :, HS : 2 * HS].astype(F32)
        query_grad = (share * SCALE) * (first - shift * second)
        query_grad += scale * unit_grad - q * (scale * scale * scale * along)
        grads.append(jnp.concatenate([query_grad, value_grad], axis=1))
    out_ref[...] = join_rounds(grads[0], grads[1]).astype(BF)


def pinned(x):
    return pltpu.with_memory_space_constraint(x, pltpu.HBM)


def backward(probs, weighted, rows, sums, mine, got):
    return pl.pallas_call(
        backward_kernel,
        grid=(HH,),
        out_shape=pltpu.HBM((ROWS, HH * 2 * HS), BF),
        in_specs=[
            SQUARE,
            SQUARE,
            pl.BlockSpec((1, RR, SLOTS, HS), lambda h: (h, 0, 0, 0)),
            pl.BlockSpec((1, RR, SLOTS, HS), lambda h: (h, 0, 0, 2)),
            WIDE,
            pl.BlockSpec((HS, SLOTS), lambda h: (0, 0)),
            pl.BlockSpec((NO * 3 * ITEMS, SLOTS), lambda h: (0, 0)),
        ],
        out_specs=pl.BlockSpec((ROWS, 2 * HS), lambda h: (0, h)),
        scratch_shapes=[
            pltpu.VMEM((SLOTS // HS, NO * 3 * ITEMS, HS), F32),
            pltpu.VMEM((HH, RR, SLOTS, 2 * HS), F32),
        ],
        compiler_params=pltpu.CompilerParams(vmem_limit_bytes=VMEM),
        name="backward",
    )(pinned(probs), pinned(weighted), pinned(rows), pinned(rows), pinned(sums), pinned(mine), got)


def collect_kernel(rows_ref, got_ref, out_ref):
    row_ids = iota((ROWS, TT), 0)
    for h in range(HH):
        first = row_ids == rows_ref[h : h + 1, :]
        second = row_ids == rows_ref[HH + h : HH + h + 1, :]
        hot = (first | second).astype(BF)
        sums = dot(hot, got_ref[:, pl.ds(h * 2 * HS, 2 * HS)], 0, 0).astype(BF)
        out_ref[0, :, pl.ds(h * HS, HS)] = sums[:, :HS]
        out_ref[1, :, pl.ds(h * HS, HS)] = sums[:, HS:]


def collect(rows, got):
    return pl.pallas_call(
        collect_kernel,
        out_shape=jax.ShapeDtypeStruct((2, TT, HH * HS), BF),
        compiler_params=pltpu.CompilerParams(vmem_limit_bytes=VMEM),
        name="collect",
    )(rows, got)


def exchange(x):
    return lax.all_to_all(x, "seq", split_axis=0, concat_axis=0, tiled=True)


def block_order(me):
    return [me, me ^ 3, me ^ 1, me ^ 2]


def blocks_of(x, me):
    size = x.shape[1] // 4
    parts = [lax.dynamic_slice_in_dim(x, i * size, size, 1) for i in block_order(me)]
    return jnp.concatenate(parts, axis=1)


def swap(x, mask):
    return lax.ppermute(x, "bkt", [(i, i ^ mask) for i in range(4)])


PARTS = 4


def per_device(tokens, weights, cotangent, buckets):
    odd = (lax.axis_index("seq") & 1).astype(jnp.int32).reshape(1)
    me = lax.axis_index("bkt")
    projected = jnp.einsum(
        "td,dcf->ctf", tokens, weights, preferred_element_type=jnp.float32
    ).astype(jnp.bfloat16)
    rows, send = dispatch(odd, buckets, projected, cotangent)
    received = exchange(send)
    rows = blocks_of(rows, me)
    probs, held, own, wire, mine = forward(received)
    everyones = exchange(wire)
    probs_t, weighted_t, sums = between(probs, held, own)
    slot_grads = exchange(backward(probs_t, weighted_t, held, sums, mine, everyones))
    grads = collect(rows, slot_grads)
    width = weights.shape[0] // PARTS
    slabs = lax.optimization_barrier(
        [weights[i * width : (i + 1) * width].transpose(1, 0, 2) for i in range(PARTS)]
    )
    sums = []
    for i, slab in enumerate(slabs):
        part = jnp.einsum("ctf,cdf->td", grads, slab, preferred_element_type=jnp.float32)
        part = part.astype(jnp.bfloat16).reshape(4, TT // 4, width)
        if i % 2 == 0:
            sums.append(part[:2] + swap(part[2:], 1))
        else:
            sums.append(
                jnp.stack([part[0], part[2]]) + swap(jnp.stack([part[1], part[3]]), 3)
            )
    outs = [x[0] + swap(x[1], 3 if i % 2 == 0 else 1) for i, x in enumerate(sums)]
    return jnp.concatenate(outs, axis=1)


def solution(mesh):
    in_specs = (P("seq", None), P(None, None, "bkt"), P("seq", "bkt"), P(None, "bkt", "seq"))
    out_specs = P(("seq", "bkt"), None)
    return jax.shard_map(
        per_device, mesh=mesh, in_specs=in_specs, out_specs=out_specs, check_vma=False
    )
```

```python
import functools
import math

import jax
import jax.numpy as jnp
from jax import lax
from jax.experimental import pallas as pl
from jax.experimental.pallas import tpu as pltpu
from jax.sharding import PartitionSpec as P

HH = 4
RR = 2
TT = 256
HS = 128
NO = 32
CAP = 12
ROWS = NO * 24
SLOTS = NO * CAP
MAIN = NO * 8
ITEMS = HH * RR
SCALE = 1.0 / math.sqrt(HS)
POWER = SCALE / math.log(2.0)
SELF_SCORE = -100000.0
FAR = -(2.0**30)
F32 = jnp.float32
BF = jnp.bfloat16
VMEM = 24 * 1024 * 1024


def iota(shape, axis):
    return lax.broadcasted_iota(jnp.int32, shape, axis)


def dot(a, b, ca=1, cb=0, precision=None):
    return lax.dot_general(
        a, b, (((ca,), (cb,)), ((), ())), preferred_element_type=F32, precision=precision
    )


def halves(x):
    high = x.astype(BF)
    return high, (x - high.astype(F32)).astype(BF)


WIRE = HH * 3 * HS + 128
OWNERS = 32
PLACES = 40
CODES = 64


def dispatch_kernel(odd_ref, buckets_ref, proj_ref, cot_ref, rows_ref, out_ref):
    odd = odd_ref[0]
    before = (iota((TT, TT), 0) < iota((TT, TT), 1)).astype(BF)
    owner_ids = iota((NO, TT), 0)
    row_ids = iota((ROWS, TT), 0)
    buckets = [buckets_ref[r, h : h + 1, :] for r in range(RR) for h in range(HH)]
    hots = [owner_ids == lax.shift_right_logical(mine, 1) for mine in buckets]
    counts = dot(jnp.concatenate([hot.astype(BF) for hot in hots], axis=0), before)
    rows, ranks = [], []
    for item in range(ITEMS):
        count = counts[item * NO : (item + 1) * NO]
        rank = jnp.sum(jnp.where(hots[item], count, 0.0), axis=0, keepdims=True)
        rank = rank.astype(jnp.int32)
        first = item // HH
        late = 4 * odd if first == 0 else 4 - 4 * odd
        row = jnp.where(rank < 8, rank + 16 * first, rank + late)
        rows.append(lax.shift_right_logical(buckets[item], 1) * 24 + row)
        ranks.append(rank)
        rows_ref[item : item + 1, :] = rows[item]
    code_ids = iota((128, TT), 0)
    marks = jnp.zeros((ROWS, 128), F32)
    for h in range(HH):
        hot = ((row_ids == rows[h]) | (row_ids == rows[HH + h])).astype(BF)
        codes = 0
        for item, other in ((h, HH + h), (HH + h, h)):
            bucket = 1 + (buckets[item] & 1)
            codes = jnp.where((code_ids >= CODES) & (code_ids & 7 == item), bucket, codes)
            owner = lax.shift_right_logical(buckets[other], 1)
            codes = jnp.where(code_ids == OWNERS + item, owner, codes)
            codes = jnp.where(code_ids == PLACES + item, ranks[other], codes)
        codes = codes.astype(F32).astype(BF)
        lanes = pl.ds(h * HS, HS)
        source = jnp.concatenate(
            [proj_ref[0, :, lanes], proj_ref[1, :, lanes], cot_ref[:, lanes]], axis=1
        )
        out_ref[:, pl.ds(h * 3 * HS, 3 * HS)] = dot(hot, source).astype(BF)
        marks += dot(hot, codes, 1, 1)
    out_ref[:, pl.ds(HH * 3 * HS, 128)] = marks.astype(BF)


def dispatch(odd, buckets, proj, cot):
    vmem = pl.BlockSpec(memory_space=pltpu.VMEM)
    return pl.pallas_call(
        dispatch_kernel,
        out_shape=(
            jax.ShapeDtypeStruct((ITEMS, TT), jnp.int32),
            jax.ShapeDtypeStruct((ROWS, WIRE), BF),
        ),
        in_specs=[pl.BlockSpec(memory_space=pltpu.SMEM), vmem, vmem, vmem],
        compiler_params=pltpu.CompilerParams(vmem_limit_bytes=VMEM),
        name="dispatch",
    )(odd, buckets, proj, cot)


def split_rounds(x):
    width = x.shape[1]
    x = x.reshape(NO, 3, 8, width)
    mixed = x[:, 1].reshape(NO // 2, 2, 8, width)
    even, odd = mixed[:, 0], mixed[:, 1]
    top = iota((NO // 2, 8, width), 1) < 4
    late0 = jnp.where(top, even, odd).reshape(SLOTS - MAIN, width)
    late1 = jnp.where(top, odd, even).reshape(SLOTS - MAIN, width)
    return (
        jnp.concatenate([x[:, 0].reshape(MAIN, width), late0], axis=0),
        jnp.concatenate([x[:, 2].reshape(MAIN, width), late1], axis=0),
    )


def join_rounds(x0, x1):
    width = x0.shape[1]
    late0 = x0[MAIN:].reshape(NO // 2, 8, width)
    late1 = x1[MAIN:].reshape(NO // 2, 8, width)
    top = iota((NO // 2, 8, width), 1) < 4
    even = jnp.where(top, late0, late1)
    odd = jnp.where(top, late1, late0)
    mixed = jnp.stack([even, odd], axis=1).reshape(NO, 1, 8, width)
    main0 = x0[:MAIN].reshape(NO, 1, 8, width)
    main1 = x1[:MAIN].reshape(NO, 1, 8, width)
    return jnp.concatenate([main0, mixed, main1], axis=1).reshape(ROWS, width)


def source_and_slot(shape, axis, which):
    row = iota(shape, axis)
    late = row - MAIN
    flip = ((late & 7) >= 4).astype(jnp.int32)
    source_late = 2 * lax.shift_right_arithmetic(late, 3) + (flip if which == 0 else 1 - flip)
    source = jnp.where(row < MAIN, lax.shift_right_logical(row, 3), source_late)
    slot = jnp.where(row < MAIN, row & 7, 8 + (late & 3))
    return source, slot


def forward_kernel(
    x_ref,
    probs_ref,
    rows_ref,
    self_ref,
    wire_ref,
    mine_ref,
    probs,
    rows,
    kept_all,
    wire,
    mine,
    bias,
    spread,
    far,
    sems,
):
    lane = iota((SLOTS, HS), 1)
    for r in range(RR):
        source_i, slot_i = source_and_slot((SLOTS, 1), 0, r)
        source_j, slot_j = source_and_slot((1, SLOTS), 1, r)
        earlier = source_j * CAP + slot_j < source_i * CAP + slot_i
        bias[r] = jnp.where(earlier, 0.0, FAR)
    for r, marks in enumerate(split_rounds(x_ref[:, pl.ds(3 * HH * HS, HS)].astype(F32))):
        held = (lane >= OWNERS) & (lane < CODES) & ((lane & 7) >> 2 == r)
        spread[r] = jnp.where(held, marks, 0.0)
        group = lane & (HS - 8)
        wanted = jnp.where(group == CODES, 1.0, jnp.where(group == CODES + 8, 2.0, 0.0))
        coded = (group >= CODES) & (group < CODES + 24)
        far[r, :, :HS] = jnp.where(coded & (marks == wanted), FAR, 0.0).astype(BF)
        other = coded & ((marks != wanted) | (group == CODES + 16))
        far[r, :, HS:] = jnp.where(other, 1.0, 0.0).astype(BF)

    copies = []
    for h in range(HH):
        rounds = split_rounds(x_ref[:, pl.ds(h * 3 * HS, 3 * HS)].astype(F32))
        for r in range(RR):
            x = rounds[r].astype(BF)
            q = rounds[r][:, :HS]
            u = rounds[r][:, 2 * HS :]
            v_half = x[:, HS : 2 * HS]
            scale = lax.rsqrt(jnp.sum(q * q, axis=1, keepdims=True) + 1e-06)
            unit = (q * scale).astype(BF)
            far_q = far[r, :, :HS] * ((lane & 7) == r * HH + h).astype(BF)
            far_k = far[r, :, HS:]
            scores = dot(
                jnp.concatenate([x[:, :HS], far_q], axis=1),
                jnp.concatenate([unit, far_k], axis=1),
                1,
                1,
            )
            scores = scores + bias[r]
            top = jnp.maximum(jnp.max(scores, axis=1, keepdims=True), SELF_SCORE / SCALE)
            shifted = jnp.exp2((scores - top) * POWER).astype(BF)
            own = jnp.exp2((SELF_SCORE / SCALE - top) * POWER)
            both = dot(shifted, jnp.concatenate([v_half, jnp.ones_like(v_half)], axis=1))
            totals = both[:, HS:] + own
            inverse = 1.0 / totals
            own = (own * inverse).astype(BF).astype(F32)
            out = both[:, :HS] * inverse + own * rounds[r][:, HS : 2 * HS]
            out = out.astype(BF).astype(F32)
            inner = jnp.sum(u * out, axis=1, keepdims=True)
            lse = top * SCALE + jnp.log(totals)
            probs[h, r] = shifted
            rows[h, r] = x
            kept = 0.0
            for at, column in enumerate((own, inner, scale, inverse)):
                kept = jnp.where(lane == at, column.astype(F32), kept)
            kept_all[h, r] = kept
            at = lane - (r * HH + h) * 3
            sent = jnp.where((at == 0) | (at == 1), lse, spread[r])
            spread[r] = jnp.where(at == 2, inner, sent)
        for at, (here, there) in enumerate(
            ((probs, probs_ref), (rows, rows_ref), (kept_all, self_ref))
        ):
            copies.append(
                pltpu.make_async_copy(here.at[h], there.at[h], sems.at[3 * h + at])
            )
            copies[-1].start()

    total = jnp.zeros((HS, SLOTS), F32)
    for r in range(RR):
        source, slot = source_and_slot((SLOTS, 1), 0, r)
        hot = (iota((SLOTS, SLOTS), 1) == slot * NO + source).astype(BF)
        high, low = halves(spread[r])
        low_lane = (lane < 3 * ITEMS) & (lane % 3 == 1)
        sent = jnp.where(low_lane, low.astype(F32), high.astype(F32)).astype(BF)
        total += dot(sent, hot, 0, 0)
    total = total.astype(BF)
    mine[...] = total
    total = total[: 3 * ITEMS]
    for k in range(NO):
        wire[pl.ds(k * 3 * ITEMS, 3 * ITEMS), :] = total
    copies += [
        pltpu.make_async_copy(mine, mine_ref, sems.at[3 * HH]),
        pltpu.make_async_copy(wire, wire_ref, sems.at[3 * HH + 1]),
    ]
    copies[-1].start()
    copies[-2].start()
    for copy in copies:
        copy.wait()


def forward(received):
    shapes = (
        ((HH, RR, SLOTS, SLOTS), BF),
        ((HH, RR, SLOTS, 3 * HS), BF),
        ((HH, RR, SLOTS, HS), F32),
        ((NO * 3 * ITEMS, SLOTS), BF),
        ((HS, SLOTS), BF),
    )
    return pl.pallas_call(
        forward_kernel,
        out_shape=tuple(pltpu.HBM(*shape) for shape in shapes),
        in_specs=[pl.BlockSpec(memory_space=pltpu.VMEM)],
        out_specs=(pl.BlockSpec(memory_space=pl.ANY),) * len(shapes),
        scratch_shapes=[pltpu.VMEM(*shape) for shape in shapes]
        + [
            pltpu.VMEM((RR, SLOTS, SLOTS), F32),
            pltpu.VMEM((RR, SLOTS, HS), F32),
            pltpu.VMEM((RR, SLOTS, 2 * HS), BF),
            pltpu.SemaphoreType.DMA((3 * HH + 2,)),
        ],
        compiler_params=pltpu.CompilerParams(vmem_limit_bytes=VMEM),
        name="forward",
    )(received)


def between_kernel(probs_ref, rows_ref, self_ref, probs_t_ref, weighted_t_ref, sums_ref):
    for r in range(RR):
        probs = (probs_ref[0, r].astype(F32) * self_ref[0, r, :, 3:4]).astype(BF)
        q = rows_ref[0, r, :, :HS]
        v = rows_ref[0, r, :, HS : 2 * HS]
        u = rows_ref[0, r, :, 2 * HS :]
        inner = self_ref[0, r, :, 1:2]
        scale = self_ref[0, r, :, 2:3]
        unit = (q.astype(F32) * scale).astype(BF)
        weighted = (probs.astype(F32) * (dot(u, v, 1, 1) - inner)).astype(BF)
        probs_t_ref[0, r] = probs.T
        weighted_t_ref[0, r] = weighted.T
        sums_ref[0, r, :, :HS] = dot(weighted, unit).astype(BF)
        sums_ref[0, r, :, HS : 2 * HS] = dot(probs, unit).astype(BF)
        own = self_ref[0, r, :, 0:1]
        sums_ref[0, r, :, 2 * HS :] = jnp.broadcast_to(own, (SLOTS, HS)).astype(BF)


SQUARE = pl.BlockSpec((1, RR, SLOTS, SLOTS), lambda h: (h, 0, 0, 0))
NARROW = pl.BlockSpec((1, RR, SLOTS, HS), lambda h: (h, 0, 0, 0))
WIDE = pl.BlockSpec((1, RR, SLOTS, 3 * HS), lambda h: (h, 0, 0, 0))


def between(probs, rows, own):
    flops = ITEMS * SLOTS * SLOTS * HS * 6
    return pl.pallas_call(
        between_kernel,
        grid=(HH,),
        out_shape=(
            pltpu.HBM((HH, RR, SLOTS, SLOTS), BF),
            pltpu.HBM((HH, RR, SLOTS, SLOTS), BF),
            pltpu.HBM((HH, RR, SLOTS, 3 * HS), BF),
        ),
        in_specs=[SQUARE, WIDE, NARROW],
        out_specs=(SQUARE, SQUARE, WIDE),
        compiler_params=pltpu.CompilerParams(vmem_limit_bytes=VMEM),
        cost_estimate=pl.CostEstimate(flops=flops, bytes_accessed=12 << 20, transcendentals=0),
        name="between",
    )(pinned(probs), pinned(rows), pinned(own))


def round_shares(mine_ref, got_ref, got, put):
    for at in range(SLOTS // HS):
        got[at] = got_ref[:, pl.ds(at * HS, HS)].astype(F32)
    mine = mine_ref[...].astype(F32)
    owner_ids = iota((3 * NO, SLOTS), 0)
    slot_ids = iota((HS, SLOTS), 0)
    source = iota((1, SLOTS), 1) & (NO - 1)
    mine_lse, mine_inner, other_lse, other_inner = [], [], [], []
    for item in range(ITEMS):
        first_row = (item ^ HH) * 3
        high, low, inners = (
            jnp.concatenate(
                [
                    got[i, pl.ds(first_row + at, NO, stride=3 * ITEMS), :]
                    for i in range(SLOTS // HS)
                ],
                axis=0,
            ).astype(BF)
            for at in range(3)
        )
        owner = mine[OWNERS + item : OWNERS + item + 1].astype(jnp.int32)
        slot = mine[PLACES + item : PLACES + item + 1].astype(jnp.int32)
        hot = (owner_ids == lax.shift_right_logical(slot, 2) * NO + owner).astype(BF)
        here = slot_ids == (slot & 3) * NO + source
        table = jnp.concatenate([high, low], axis=0)
        logs = dot(table, jnp.concatenate([hot, hot], axis=0), 0, 0)
        inners = dot(inners, hot, 0, 0)
        other_lse.append(jnp.sum(jnp.where(here, logs, 0.0), axis=0, keepdims=True))
        other_inner.append(jnp.sum(jnp.where(here, inners, 0.0), axis=0, keepdims=True))
        mine_lse.append(mine[item * 3 : item * 3 + 1] + mine[item * 3 + 1 : item * 3 + 2])
        mine_inner.append(mine[item * 3 + 2 : item * 3 + 3])
    mine_lse, mine_inner, other_lse, other_inner = (
        jnp.concatenate(x, axis=0) for x in (mine_lse, mine_inner, other_lse, other_inner)
    )
    top = jnp.maximum(mine_lse, other_lse)
    share = jnp.exp(mine_lse - top)
    other_share = jnp.exp(other_lse - top)
    inverse = 1.0 / (share + other_share)
    share = share * inverse
    shift = other_share * inverse * (other_inner - mine_inner)
    high, low = halves(jnp.concatenate([share, shift], axis=0))
    both = jnp.concatenate([high, low], axis=1)
    for r in range(RR):
        source, slot = source_and_slot((SLOTS, 1), 0, r)
        hot = (iota((SLOTS, SLOTS), 1) == slot * NO + source).astype(BF)
        columns = dot(jnp.concatenate([hot, hot], axis=1), both, 1, 1)
        for h in range(HH):
            item = r * HH + h
            put[h, r, :, :HS] = jnp.broadcast_to(columns[:, item : item + 1], (SLOTS, HS))
            item += ITEMS
            put[h, r, :, HS:] = jnp.broadcast_to(columns[:, item : item + 1], (SLOTS, HS))


def backward_kernel(
    probs_ref,
    weighted_ref,
    rows_ref,
    sums_ref,
    mine_ref,
    got_ref,
    out_ref,
    probs,
    weighted,
    queries,
    upstream,
    sums,
    out,
    got,
    put,
    sems,
):
    loads = []
    for h in range(HH):
        pairs = (
            (probs_ref.at[h], probs.at[h]),
            (weighted_ref.at[h], weighted.at[h]),
            (rows_ref.at[h, :, :, pl.ds(0, HS)], queries.at[h]),
            (rows_ref.at[h, :, :, pl.ds(2 * HS, HS)], upstream.at[h]),
            (sums_ref.at[h], sums.at[h]),
        )
        loads.append(
            [pltpu.make_async_copy(*p, sems.at[6 * h + at]) for at, p in enumerate(pairs)]
        )
        for copy in loads[h]:
            copy.start()
    round_shares(mine_ref, got_ref, got, put)
    stores = []
    for h in range(HH):
        for copy in loads[h]:
            copy.wait()
        grads = []
        for r in range(RR):
            share = put[h, r, :, :HS]
            shift = put[h, r, :, HS:]
            q = queries[h, r].astype(F32)
            u_share = share * upstream[h, r].astype(F32)
            q_share = share * q
            right = jnp.concatenate([-shift * q_share, u_share], axis=1).astype(BF)
            both = dot(probs[h, r], right)
            unit_grad = (dot(weighted[h, r], q_share.astype(BF)) + both[:, :HS]) * SCALE
            value_grad = both[:, HS:] + sums[h, r, :, 2 * HS :].astype(F32) * u_share
            scale = lax.rsqrt(jnp.sum(q * q, axis=1, keepdims=True) + 1e-06)
            along = jnp.sum(q * unit_grad, axis=1, keepdims=True)
            first = sums[h, r, :, :HS].astype(F32)
            second = sums[h, r, :, HS : 2 * HS].astype(F32)
            query_grad = (share * SCALE) * (first - shift * second)
            query_grad += scale * unit_grad - q * (scale * scale * scale * along)
            grads.append(jnp.concatenate([query_grad, value_grad], axis=1))
        out[h] = join_rounds(grads[0], grads[1]).astype(BF)
        there = out_ref.at[:, pl.ds(h * 2 * HS, 2 * HS)]
        stores.append(pltpu.make_async_copy(out.at[h], there, sems.at[6 * h + 5]))
        stores[h].start()
    for copy in stores:
        copy.wait()


def pinned(x):
    return pltpu.with_memory_space_constraint(x, pltpu.HBM)


def backward(probs, weighted, rows, sums, mine, got):
    hbm = pl.BlockSpec(memory_space=pl.ANY)
    vmem = pl.BlockSpec(memory_space=pltpu.VMEM)
    return pl.pallas_call(
        backward_kernel,
        out_shape=pltpu.HBM((ROWS, HH * 2 * HS), BF),
        in_specs=[hbm, hbm, hbm, hbm, vmem, vmem],
        out_specs=hbm,
        scratch_shapes=[
            pltpu.VMEM((HH, RR, SLOTS, SLOTS), BF),
            pltpu.VMEM((HH, RR, SLOTS, SLOTS), BF),
            pltpu.VMEM((HH, RR, SLOTS, HS), BF),
            pltpu.VMEM((HH, RR, SLOTS, HS), BF),
            pltpu.VMEM((HH, RR, SLOTS, 3 * HS), BF),
            pltpu.VMEM((HH, ROWS, 2 * HS), BF),
            pltpu.VMEM((SLOTS // HS, NO * 3 * ITEMS, HS), F32),
            pltpu.VMEM((HH, RR, SLOTS, 2 * HS), F32),
            pltpu.SemaphoreType.DMA((6 * HH,)),
        ],
        compiler_params=pltpu.CompilerParams(vmem_limit_bytes=VMEM),
        name="backward",
    )(pinned(probs), pinned(weighted), pinned(rows), pinned(sums), mine, got)


def collect_kernel(rows_ref, got_ref, out_ref, got, sems):
    loads = []
    for h in range(HH):
        here = got_ref.at[:, pl.ds(h * 2 * HS, 2 * HS)]
        loads.append(pltpu.make_async_copy(here, got.at[h], sems.at[h]))
        loads[h].start()
    row_ids = iota((TT, ROWS), 1)
    for h in range(HH):
        first = row_ids == rows_ref[:, h : h + 1]
        second = row_ids == rows_ref[:, HH + h : HH + h + 1]
        hot = (first | second).astype(BF)
        loads[h].wait()
        sums = dot(hot, got[h]).astype(BF)
        out_ref[0, :, pl.ds(h * HS, HS)] = sums[:, :HS]
        out_ref[1, :, pl.ds(h * HS, HS)] = sums[:, HS:]


def collect(rows, got):
    return pl.pallas_call(
        collect_kernel,
        out_shape=jax.ShapeDtypeStruct((2, TT, HH * HS), BF),
        in_specs=[pl.BlockSpec(memory_space=pltpu.VMEM), pl.BlockSpec(memory_space=pl.ANY)],
        out_specs=pl.BlockSpec(memory_space=pltpu.VMEM),
        scratch_shapes=[
            pltpu.VMEM((HH, ROWS, 2 * HS), BF),
            pltpu.SemaphoreType.DMA((HH,)),
        ],
        compiler_params=pltpu.CompilerParams(vmem_limit_bytes=VMEM),
        name="collect",
    )(rows, pinned(got))


def exchange(x):
    return lax.all_to_all(x, "seq", split_axis=0, concat_axis=0, tiled=True)


def block_order(me):
    return [me, me ^ 3, me ^ 1, me ^ 2]


def blocks_of(x, me):
    size = x.shape[1] // 4
    parts = [lax.dynamic_slice_in_dim(x, i * size, size, 1) for i in block_order(me)]
    return jnp.concatenate(parts, axis=1)


def swap(x, mask):
    return lax.ppermute(x, "bkt", [(i, i ^ mask) for i in range(4)])


PARTS = 4


def per_device(tokens, weights, cotangent, buckets):
    odd = (lax.axis_index("seq") & 1).astype(jnp.int32).reshape(1)
    me = lax.axis_index("bkt")
    projected = jnp.einsum(
        "td,dcf->ctf", tokens, weights, preferred_element_type=jnp.float32
    ).astype(jnp.bfloat16)
    rows, send = dispatch(odd, buckets, projected, cotangent)
    received = exchange(send)
    rows = blocks_of(rows, me).T
    probs, held, own, wire, mine = forward(received)
    everyones = exchange(wire)
    probs_t, weighted_t, sums = between(probs, held, own)
    slot_grads = exchange(backward(probs_t, weighted_t, held, sums, mine, everyones))
    grads = collect(rows, slot_grads)
    width = weights.shape[0] // PARTS
    slabs = lax.optimization_barrier(
        [weights[i * width : (i + 1) * width].transpose(1, 0, 2) for i in range(PARTS)]
    )
    sums = []
    for i, slab in enumerate(slabs):
        part = jnp.einsum("ctf,cdf->td", grads, slab, preferred_element_type=jnp.float32)
        part = part.astype(jnp.bfloat16).reshape(4, TT // 4, width)
        if i % 2 == 0:
            sums.append(part[:2] + swap(part[2:], 1))
        else:
            sums.append(
                jnp.stack([part[0], part[2]]) + swap(jnp.stack([part[1], part[3]]), 3)
            )
    outs = [x[0] + swap(x[1], 3 if i % 2 == 0 else 1) for i, x in enumerate(sums)]
    return jnp.concatenate(outs, axis=1)


def solution(mesh):
    in_specs = (P("seq", None), P(None, None, "bkt"), P("seq", "bkt"), P(None, "bkt", "seq"))
    out_specs = P(("seq", "bkt"), None)
    return jax.shard_map(
        per_device, mesh=mesh, in_specs=in_specs, out_specs=out_specs, check_vma=False
    )
```

```python
import functools
import math

import jax
import jax.numpy as jnp
from jax import lax
from jax.experimental import pallas as pl
from jax.experimental.pallas import tpu as pltpu
from jax.sharding import PartitionSpec as P

HH = 4
RR = 2
TT = 256
HS = 128
NO = 32
CAP = 12
ROWS = NO * 24
SLOTS = NO * CAP
MAIN = NO * 8
ITEMS = HH * RR
SCALE = 1.0 / math.sqrt(HS)
POWER = SCALE / math.log(2.0)
SELF_SCORE = -100000.0
FAR = -(2.0**30)
LSE_SHIFT = 4.5
F32 = jnp.float32
BF = jnp.bfloat16
VMEM = 24 * 1024 * 1024


def iota(shape, axis):
    return lax.broadcasted_iota(jnp.int32, shape, axis)


def dot(a, b, ca=1, cb=0, precision=None):
    return lax.dot_general(
        a, b, (((ca,), (cb,)), ((), ())), preferred_element_type=F32, precision=precision
    )


def halves(x):
    high = x.astype(BF)
    return high, (x - high.astype(F32)).astype(BF)


WIRE = HH * 3 * HS + 128
OWNERS = 32
PLACES = 40
CODES = 64


def dispatch_kernel(odd_ref, buckets_ref, proj_ref, cot_ref, rows_ref, out_ref):
    odd = odd_ref[0]
    before = (iota((TT, TT), 0) < iota((TT, TT), 1)).astype(BF)
    owner_ids = iota((NO, TT), 0)
    row_ids = iota((ROWS, TT), 0)
    buckets = [buckets_ref[r, h : h + 1, :] for r in range(RR) for h in range(HH)]
    hots = [owner_ids == lax.shift_right_logical(mine, 1) for mine in buckets]
    counts = dot(jnp.concatenate([hot.astype(BF) for hot in hots], axis=0), before)
    rows, ranks = [], []
    for item in range(ITEMS):
        count = counts[item * NO : (item + 1) * NO]
        rank = jnp.sum(jnp.where(hots[item], count, 0.0), axis=0, keepdims=True)
        rank = rank.astype(jnp.int32)
        first = item // HH
        late = 4 * odd if first == 0 else 4 - 4 * odd
        row = jnp.where(rank < 8, rank + 16 * first, rank + late)
        rows.append(lax.shift_right_logical(buckets[item], 1) * 24 + row)
        ranks.append(rank)
        rows_ref[item : item + 1, :] = rows[item]
    code_ids = iota((128, TT), 0)
    marks = jnp.zeros((ROWS, 128), F32)
    for h in range(HH):
        hot = ((row_ids == rows[h]) | (row_ids == rows[HH + h])).astype(BF)
        codes = 0
        for item, other in ((h, HH + h), (HH + h, h)):
            bucket = 1 + (buckets[item] & 1)
            codes = jnp.where((code_ids >= CODES) & (code_ids & 7 == item), bucket, codes)
            owner = lax.shift_right_logical(buckets[other], 1)
            codes = jnp.where(code_ids == OWNERS + item, owner, codes)
            codes = jnp.where(code_ids == PLACES + item, ranks[other], codes)
        codes = codes.astype(F32).astype(BF)
        lanes = pl.ds(h * HS, HS)
        source = jnp.concatenate(
            [proj_ref[0, :, lanes], proj_ref[1, :, lanes], cot_ref[:, lanes]], axis=1
        )
        out_ref[:, pl.ds(h * 3 * HS, 3 * HS)] = dot(hot, source).astype(BF)
        marks += dot(hot, codes, 1, 1)
    out_ref[:, pl.ds(HH * 3 * HS, 128)] = marks.astype(BF)


def dispatch(odd, buckets, proj, cot):
    vmem = pl.BlockSpec(memory_space=pltpu.VMEM)
    return pl.pallas_call(
        dispatch_kernel,
        out_shape=(
            jax.ShapeDtypeStruct((ITEMS, TT), jnp.int32),
            jax.ShapeDtypeStruct((ROWS, WIRE), BF),
        ),
        in_specs=[pl.BlockSpec(memory_space=pltpu.SMEM), vmem, vmem, vmem],
        compiler_params=pltpu.CompilerParams(vmem_limit_bytes=VMEM),
        name="dispatch",
    )(odd, buckets, proj, cot)


def split_rounds(x):
    width = x.shape[1]
    x = x.reshape(NO, 3, 8, width)
    mixed = x[:, 1].reshape(NO // 2, 2, 8, width)
    even, odd = mixed[:, 0], mixed[:, 1]
    top = iota((NO // 2, 8, width), 1) < 4
    late0 = jnp.where(top, even, odd).reshape(SLOTS - MAIN, width)
    late1 = jnp.where(top, odd, even).reshape(SLOTS - MAIN, width)
    return (
        jnp.concatenate([x[:, 0].reshape(MAIN, width), late0], axis=0),
        jnp.concatenate([x[:, 2].reshape(MAIN, width), late1], axis=0),
    )


def join_rounds(x0, x1):
    width = x0.shape[1]
    late0 = x0[MAIN:].reshape(NO // 2, 8, width)
    late1 = x1[MAIN:].reshape(NO // 2, 8, width)
    top = iota((NO // 2, 8, width), 1) < 4
    even = jnp.where(top, late0, late1)
    odd = jnp.where(top, late1, late0)
    mixed = jnp.stack([even, odd], axis=1).reshape(NO, 1, 8, width)
    main0 = x0[:MAIN].reshape(NO, 1, 8, width)
    main1 = x1[:MAIN].reshape(NO, 1, 8, width)
    return jnp.concatenate([main0, mixed, main1], axis=1).reshape(ROWS, width)


def source_and_slot(shape, axis, which):
    row = iota(shape, axis)
    late = row - MAIN
    flip = ((late & 7) >= 4).astype(jnp.int32)
    source_late = 2 * lax.shift_right_arithmetic(late, 3) + (flip if which == 0 else 1 - flip)
    source = jnp.where(row < MAIN, lax.shift_right_logical(row, 3), source_late)
    slot = jnp.where(row < MAIN, row & 7, 8 + (late & 3))
    return source, slot


def forward_kernel(
    x_ref,
    probs_ref,
    rows_ref,
    self_ref,
    wire_ref,
    mine_ref,
    probs,
    rows,
    kept_all,
    wire,
    mine,
    bias,
    spread,
    far,
    sems,
):
    lane = iota((SLOTS, HS), 1)
    for r in range(RR):
        source_i, slot_i = source_and_slot((SLOTS, 1), 0, r)
        source_j, slot_j = source_and_slot((1, SLOTS), 1, r)
        earlier = source_j * CAP + slot_j < source_i * CAP + slot_i
        bias[r] = jnp.where(earlier, 0.0, FAR)
    for r, marks in enumerate(split_rounds(x_ref[:, pl.ds(3 * HH * HS, HS)].astype(F32))):
        held = (lane >= OWNERS) & (lane < CODES) & ((lane & 7) >> 2 == r)
        spread[r] = jnp.where(held, marks, 0.0)
        group = lane & (HS - 8)
        wanted = jnp.where(group == CODES, 1.0, jnp.where(group == CODES + 8, 2.0, 0.0))
        coded = (group >= CODES) & (group < CODES + 24)
        far[r, :, :HS] = jnp.where(coded & (marks == wanted), FAR, 0.0).astype(BF)
        other = coded & ((marks != wanted) | (group == CODES + 16))
        far[r, :, HS:] = jnp.where(other, 1.0, 0.0).astype(BF)

    copies = []
    for h in range(HH):
        rounds = split_rounds(x_ref[:, pl.ds(h * 3 * HS, 3 * HS)].astype(F32))
        for r in range(RR):
            x = rounds[r].astype(BF)
            q = rounds[r][:, :HS]
            u = rounds[r][:, 2 * HS :]
            v_half = x[:, HS : 2 * HS]
            scale = lax.rsqrt(jnp.sum(q * q, axis=1, keepdims=True) + 1e-06)
            unit = (q * scale).astype(BF)
            far_q = far[r, :, :HS] * ((lane & 7) == r * HH + h).astype(BF)
            far_k = far[r, :, HS:]
            scores = dot(
                jnp.concatenate([x[:, :HS], far_q], axis=1),
                jnp.concatenate([unit, far_k], axis=1),
                1,
                1,
            )
            scores = scores + bias[r]
            top = jnp.maximum(jnp.max(scores, axis=1, keepdims=True), SELF_SCORE / SCALE)
            shifted = jnp.exp2((scores - top) * POWER).astype(BF)
            own = jnp.exp2((SELF_SCORE / SCALE - top) * POWER)
            both = dot(shifted, jnp.concatenate([v_half, jnp.ones_like(v_half)], axis=1))
            totals = both[:, HS:] + own
            inverse = 1.0 / totals
            own = (own * inverse).astype(BF).astype(F32)
            out = both[:, :HS] * inverse + own * rounds[r][:, HS : 2 * HS]
            out = out.astype(BF).astype(F32)
            inner = jnp.sum(u * out, axis=1, keepdims=True)
            lse = top * SCALE + jnp.log(totals)
            probs[h, r] = shifted
            rows[h, r] = x
            kept = 0.0
            for at, column in enumerate((own, inner, scale, inverse)):
                kept = jnp.where(lane == at, column.astype(F32), kept)
            kept_all[h, r] = kept
            at = lane - (r * HH + h) * 2
            sent = jnp.where(at == 0, lse - LSE_SHIFT, spread[r])
            spread[r] = jnp.where(at == 1, inner, sent)
        for at, (here, there) in enumerate(
            ((probs, probs_ref), (rows, rows_ref), (kept_all, self_ref))
        ):
            copies.append(
                pltpu.make_async_copy(here.at[h], there.at[h], sems.at[3 * h + at])
            )
            copies[-1].start()

    total = jnp.zeros((HS, SLOTS), F32)
    for r in range(RR):
        source, slot = source_and_slot((SLOTS, 1), 0, r)
        hot = (iota((SLOTS, SLOTS), 1) == slot * NO + source).astype(BF)
        total += dot(spread[r].astype(BF), hot, 0, 0)
    total = total.astype(BF)
    mine[...] = total
    total = total[: 2 * ITEMS]
    for k in range(NO):
        wire[pl.ds(k * 2 * ITEMS, 2 * ITEMS), :] = total
    copies += [
        pltpu.make_async_copy(mine, mine_ref, sems.at[3 * HH]),
        pltpu.make_async_copy(wire, wire_ref, sems.at[3 * HH + 1]),
    ]
    copies[-1].start()
    copies[-2].start()
    for copy in copies:
        copy.wait()


def forward(received):
    shapes = (
        ((HH, RR, SLOTS, SLOTS), BF),
        ((HH, RR, SLOTS, 3 * HS), BF),
        ((HH, RR, SLOTS, HS), F32),
        ((NO * 2 * ITEMS, SLOTS), BF),
        ((HS, SLOTS), BF),
    )
    return pl.pallas_call(
        forward_kernel,
        out_shape=tuple(pltpu.HBM(*shape) for shape in shapes),
        in_specs=[pl.BlockSpec(memory_space=pltpu.VMEM)],
        out_specs=(pl.BlockSpec(memory_space=pl.ANY),) * len(shapes),
        scratch_shapes=[pltpu.VMEM(*shape) for shape in shapes]
        + [
            pltpu.VMEM((RR, SLOTS, SLOTS), F32),
            pltpu.VMEM((RR, SLOTS, HS), F32),
            pltpu.VMEM((RR, SLOTS, 2 * HS), BF),
            pltpu.SemaphoreType.DMA((3 * HH + 2,)),
        ],
        compiler_params=pltpu.CompilerParams(vmem_limit_bytes=VMEM),
        name="forward",
    )(received)


def between_kernel(probs_ref, rows_ref, self_ref, probs_t_ref, weighted_t_ref, sums_ref):
    for r in range(RR):
        probs = (probs_ref[0, r].astype(F32) * self_ref[0, r, :, 3:4]).astype(BF)
        q = rows_ref[0, r, :, :HS]
        v = rows_ref[0, r, :, HS : 2 * HS]
        u = rows_ref[0, r, :, 2 * HS :]
        inner = self_ref[0, r, :, 1:2]
        scale = self_ref[0, r, :, 2:3]
        unit = (q.astype(F32) * scale).astype(BF)
        weighted = (probs.astype(F32) * (dot(u, v, 1, 1) - inner)).astype(BF)
        probs_t_ref[0, r] = probs.T
        weighted_t_ref[0, r] = weighted.T
        sums_ref[0, r, :, :HS] = dot(weighted, unit).astype(BF)
        sums_ref[0, r, :, HS : 2 * HS] = dot(probs, unit).astype(BF)
        own = self_ref[0, r, :, 0:1]
        sums_ref[0, r, :, 2 * HS :] = jnp.broadcast_to(own, (SLOTS, HS)).astype(BF)


SQUARE = pl.BlockSpec((1, RR, SLOTS, SLOTS), lambda h: (h, 0, 0, 0))
NARROW = pl.BlockSpec((1, RR, SLOTS, HS), lambda h: (h, 0, 0, 0))
WIDE = pl.BlockSpec((1, RR, SLOTS, 3 * HS), lambda h: (h, 0, 0, 0))


def between(probs, rows, own):
    flops = ITEMS * SLOTS * SLOTS * HS * 6
    return pl.pallas_call(
        between_kernel,
        grid=(HH,),
        out_shape=(
            pltpu.HBM((HH, RR, SLOTS, SLOTS), BF),
            pltpu.HBM((HH, RR, SLOTS, SLOTS), BF),
            pltpu.HBM((HH, RR, SLOTS, 3 * HS), BF),
        ),
        in_specs=[SQUARE, WIDE, NARROW],
        out_specs=(SQUARE, SQUARE, WIDE),
        compiler_params=pltpu.CompilerParams(vmem_limit_bytes=VMEM),
        cost_estimate=pl.CostEstimate(flops=flops, bytes_accessed=12 << 20, transcendentals=0),
        name="between",
    )(pinned(probs), pinned(rows), pinned(own))


def round_shares(mine_ref, got_ref, got, put):
    for at in range(SLOTS // HS):
        got[at] = got_ref[:, pl.ds(at * HS, HS)].astype(F32)
    mine = mine_ref[...].astype(F32)
    owner_ids = iota((3 * NO, SLOTS), 0)
    slot_ids = iota((HS, SLOTS), 0)
    source = iota((1, SLOTS), 1) & (NO - 1)
    mine_lse, mine_inner, other_lse, other_inner = [], [], [], []
    for item in range(ITEMS):
        first_row = (item ^ HH) * 2
        table = jnp.concatenate(
            [
                jnp.concatenate(
                    [
                        got[i, pl.ds(first_row + at, NO, stride=2 * ITEMS), :]
                        for i in range(SLOTS // HS)
                    ],
                    axis=0,
                ).astype(BF)
                for at in range(2)
            ],
            axis=1,
        )
        owner = mine[OWNERS + item : OWNERS + item + 1].astype(jnp.int32)
        slot = mine[PLACES + item : PLACES + item + 1].astype(jnp.int32)
        hot = (owner_ids == lax.shift_right_logical(slot, 2) * NO + owner).astype(BF)
        here = slot_ids == (slot & 3) * NO + source
        seen = dot(table, hot, 0, 0)
        other_lse.append(jnp.sum(jnp.where(here, seen[:HS], 0.0), axis=0, keepdims=True))
        other_inner.append(jnp.sum(jnp.where(here, seen[HS:], 0.0), axis=0, keepdims=True))
        mine_lse.append(mine[item * 2 : item * 2 + 1])
        mine_inner.append(mine[item * 2 + 1 : item * 2 + 2])
    mine_lse, mine_inner, other_lse, other_inner = (
        jnp.concatenate(x, axis=0) for x in (mine_lse, mine_inner, other_lse, other_inner)
    )
    top = jnp.maximum(mine_lse, other_lse)
    share = jnp.exp(mine_lse - top)
    other_share = jnp.exp(other_lse - top)
    inverse = 1.0 / (share + other_share)
    share = share * inverse
    shift = other_share * inverse * (other_inner - mine_inner)
    high, low = halves(jnp.concatenate([share, shift], axis=0))
    both = jnp.concatenate([high, low], axis=1)
    for r in range(RR):
        source, slot = source_and_slot((SLOTS, 1), 0, r)
        hot = (iota((SLOTS, SLOTS), 1) == slot * NO + source).astype(BF)
        columns = dot(jnp.concatenate([hot, hot], axis=1), both, 1, 1)
        for h in range(HH):
            item = r * HH + h
            put[h, r, :, :HS] = jnp.broadcast_to(columns[:, item : item + 1], (SLOTS, HS))
            item += ITEMS
            put[h, r, :, HS:] = jnp.broadcast_to(columns[:, item : item + 1], (SLOTS, HS))


def backward_kernel(
    probs_ref,
    weighted_ref,
    rows_ref,
    sums_ref,
    mine_ref,
    got_ref,
    out_ref,
    probs,
    weighted,
    queries,
    upstream,
    sums,
    out,
    got,
    put,
    sems,
):
    loads = []
    for h in range(HH):
        pairs = (
            (probs_ref.at[h], probs.at[h]),
            (weighted_ref.at[h], weighted.at[h]),
            (rows_ref.at[h, :, :, pl.ds(0, HS)], queries.at[h]),
            (rows_ref.at[h, :, :, pl.ds(2 * HS, HS)], upstream.at[h]),
            (sums_ref.at[h], sums.at[h]),
        )
        loads.append(
            [pltpu.make_async_copy(*p, sems.at[6 * h + at]) for at, p in enumerate(pairs)]
        )
        for copy in loads[h]:
            copy.start()
    round_shares(mine_ref, got_ref, got, put)
    stores = []
    for h in range(HH):
        for copy in loads[h]:
            copy.wait()
        grads = []
        for r in range(RR):
            share = put[h, r, :, :HS]
            shift = put[h, r, :, HS:]
            q = queries[h, r].astype(F32)
            u_share = share * upstream[h, r].astype(F32)
            q_share = share * q
            right = jnp.concatenate([-shift * q_share, u_share], axis=1).astype(BF)
            both = dot(probs[h, r], right)
            unit_grad = (dot(weighted[h, r], q_share.astype(BF)) + both[:, :HS]) * SCALE
            value_grad = both[:, HS:] + sums[h, r, :, 2 * HS :].astype(F32) * u_share
            scale = lax.rsqrt(jnp.sum(q * q, axis=1, keepdims=True) + 1e-06)
            along = jnp.sum(q * unit_grad, axis=1, keepdims=True)
            first = sums[h, r, :, :HS].astype(F32)
            second = sums[h, r, :, HS : 2 * HS].astype(F32)
            query_grad = (share * SCALE) * (first - shift * second)
            query_grad += scale * unit_grad - q * (scale * scale * scale * along)
            grads.append(jnp.concatenate([query_grad, value_grad], axis=1))
        out[h] = join_rounds(grads[0], grads[1]).astype(BF)
        there = out_ref.at[:, pl.ds(h * 2 * HS, 2 * HS)]
        stores.append(pltpu.make_async_copy(out.at[h], there, sems.at[6 * h + 5]))
        stores[h].start()
    for copy in stores:
        copy.wait()


def pinned(x):
    return pltpu.with_memory_space_constraint(x, pltpu.HBM)


def backward(probs, weighted, rows, sums, mine, got):
    hbm = pl.BlockSpec(memory_space=pl.ANY)
    vmem = pl.BlockSpec(memory_space=pltpu.VMEM)
    return pl.pallas_call(
        backward_kernel,
        out_shape=pltpu.HBM((ROWS, HH * 2 * HS), BF),
        in_specs=[hbm, hbm, hbm, hbm, vmem, vmem],
        out_specs=hbm,
        scratch_shapes=[
            pltpu.VMEM((HH, RR, SLOTS, SLOTS), BF),
            pltpu.VMEM((HH, RR, SLOTS, SLOTS), BF),
            pltpu.VMEM((HH, RR, SLOTS, HS), BF),
            pltpu.VMEM((HH, RR, SLOTS, HS), BF),
            pltpu.VMEM((HH, RR, SLOTS, 3 * HS), BF),
            pltpu.VMEM((HH, ROWS, 2 * HS), BF),
            pltpu.VMEM((SLOTS // HS, NO * 2 * ITEMS, HS), F32),
            pltpu.VMEM((HH, RR, SLOTS, 2 * HS), F32),
            pltpu.SemaphoreType.DMA((6 * HH,)),
        ],
        compiler_params=pltpu.CompilerParams(vmem_limit_bytes=VMEM),
        name="backward",
    )(pinned(probs), pinned(weighted), pinned(rows), pinned(sums), mine, got)


def collect_kernel(rows_ref, got_ref, out_ref, got, sems):
    loads = []
    for at in range(3):
        part = pl.ds(at * (ROWS // 3), ROWS // 3)
        loads.append(pltpu.make_async_copy(got_ref.at[part], got.at[part], sems.at[at]))
        loads[at].start()
    row_ids = iota((TT, ROWS), 1)
    hots = []
    for h in range(HH):
        first = row_ids == rows_ref[:, h : h + 1]
        second = row_ids == rows_ref[:, HH + h : HH + h + 1]
        hots.append((first | second).astype(BF))
    for copy in loads:
        copy.wait()
    for h in range(HH):
        sums = dot(hots[h], got[:, pl.ds(h * 2 * HS, 2 * HS)]).astype(BF)
        out_ref[0, :, pl.ds(h * HS, HS)] = sums[:, :HS]
        out_ref[1, :, pl.ds(h * HS, HS)] = sums[:, HS:]


def collect(rows, got):
    return pl.pallas_call(
        collect_kernel,
        out_shape=jax.ShapeDtypeStruct((2, TT, HH * HS), BF),
        in_specs=[pl.BlockSpec(memory_space=pltpu.VMEM), pl.BlockSpec(memory_space=pl.ANY)],
        out_specs=pl.BlockSpec(memory_space=pltpu.VMEM),
        scratch_shapes=[
            pltpu.VMEM((ROWS, HH * 2 * HS), BF),
            pltpu.SemaphoreType.DMA((3,)),
        ],
        compiler_params=pltpu.CompilerParams(vmem_limit_bytes=VMEM),
        name="collect",
    )(rows, pinned(got))


def exchange(x):
    return lax.all_to_all(x, "seq", split_axis=0, concat_axis=0, tiled=True)


def block_order(me):
    return [me, me ^ 3, me ^ 1, me ^ 2]


def blocks_of(x, me):
    size = x.shape[1] // 4
    parts = [lax.dynamic_slice_in_dim(x, i * size, size, 1) for i in block_order(me)]
    return jnp.concatenate(parts, axis=1)


def swap(x, mask):
    return lax.ppermute(x, "bkt", [(i, i ^ mask) for i in range(4)])


PARTS = 4


def per_device(tokens, weights, cotangent, buckets):
    odd = (lax.axis_index("seq") & 1).astype(jnp.int32).reshape(1)
    me = lax.axis_index("bkt")
    projected = jnp.einsum(
        "td,dcf->ctf", tokens, weights, preferred_element_type=jnp.float32
    ).astype(jnp.bfloat16)
    rows, send = dispatch(odd, buckets, projected, cotangent)
    received = exchange(send)
    rows = blocks_of(rows, me).T
    probs, held, own, wire, mine = forward(received)
    everyones = exchange(wire)
    probs_t, weighted_t, sums = between(probs, held, own)
    slot_grads = exchange(backward(probs_t, weighted_t, held, sums, mine, everyones))
    grads = collect(rows, slot_grads)
    width = weights.shape[0] // PARTS
    slabs = lax.optimization_barrier(
        [weights[i * width : (i + 1) * width].transpose(1, 0, 2) for i in range(PARTS)]
    )
    sums = []
    for i, slab in enumerate(slabs):
        part = jnp.einsum("ctf,cdf->td", grads, slab, preferred_element_type=jnp.float32)
        part = part.astype(jnp.bfloat16).reshape(4, TT // 4, width)
        if i % 2 == 0:
            sums.append(part[:2] + swap(part[2:], 1))
        else:
            sums.append(
                jnp.stack([part[0], part[2]]) + swap(jnp.stack([part[1], part[3]]), 3)
            )
    outs = [x[0] + swap(x[1], 3 if i % 2 == 0 else 1) for i, x in enumerate(sums)]
    return jnp.concatenate(outs, axis=1)


def solution(mesh):
    in_specs = (P("seq", None), P(None, None, "bkt"), P("seq", "bkt"), P(None, "bkt", "seq"))
    out_specs = P(("seq", "bkt"), None)
    return jax.shard_map(
        per_device, mesh=mesh, in_specs=in_specs, out_specs=out_specs, check_vma=False
    )
```

```python
import functools
import math

import jax
import jax.numpy as jnp
from jax import lax
from jax.experimental import pallas as pl
from jax.experimental.pallas import tpu as pltpu
from jax.sharding import PartitionSpec as P

HH = 4
RR = 2
TT = 256
HS = 128
NO = 32
CAP = 12
ROWS = NO * 24
SLOTS = NO * CAP
MAIN = NO * 8
ITEMS = HH * RR
SCALE = 1.0 / math.sqrt(HS)
POWER = SCALE / math.log(2.0)
SELF_SCORE = -100000.0
FAR = -(2.0**30)
LSE_SHIFT = 4.5
F32 = jnp.float32
BF = jnp.bfloat16
VMEM = 24 * 1024 * 1024


def iota(shape, axis):
    return lax.broadcasted_iota(jnp.int32, shape, axis)


def dot(a, b, ca=1, cb=0, precision=None):
    return lax.dot_general(
        a, b, (((ca,), (cb,)), ((), ())), preferred_element_type=F32, precision=precision
    )


def halves(x):
    high = x.astype(BF)
    return high, (x - high.astype(F32)).astype(BF)


WIRE = HH * 3 * HS + 128
OWNERS = 32
PLACES = 40
CODES = 64


def dispatch_kernel(odd_ref, buckets_ref, proj_ref, cot_ref, rows_ref, out_ref):
    odd = odd_ref[0]
    before = (iota((TT, TT), 0) < iota((TT, TT), 1)).astype(BF)
    owner_ids = iota((NO, TT), 0)
    row_ids = iota((ROWS, TT), 0)
    buckets = [buckets_ref[r, h : h + 1, :] for r in range(RR) for h in range(HH)]
    hots = [owner_ids == lax.shift_right_logical(mine, 1) for mine in buckets]
    counts = dot(jnp.concatenate([hot.astype(BF) for hot in hots], axis=0), before)
    rows, ranks = [], []
    for item in range(ITEMS):
        count = counts[item * NO : (item + 1) * NO]
        rank = jnp.sum(jnp.where(hots[item], count, 0.0), axis=0, keepdims=True)
        rank = rank.astype(jnp.int32)
        first = item // HH
        late = 4 * odd if first == 0 else 4 - 4 * odd
        row = jnp.where(rank < 8, rank + 16 * first, rank + late)
        rows.append(lax.shift_right_logical(buckets[item], 1) * 24 + row)
        ranks.append(rank)
        rows_ref[item : item + 1, :] = rows[item]
    code_ids = iota((128, TT), 0)
    marks = jnp.zeros((ROWS, 128), F32)
    for h in range(HH):
        hot = ((row_ids == rows[h]) | (row_ids == rows[HH + h])).astype(BF)
        codes = 0
        for item, other in ((h, HH + h), (HH + h, h)):
            bucket = 1 + (buckets[item] & 1)
            codes = jnp.where((code_ids >= CODES) & (code_ids & 7 == item), bucket, codes)
            owner = lax.shift_right_logical(buckets[other], 1)
            codes = jnp.where(code_ids == OWNERS + item, owner, codes)
            codes = jnp.where(code_ids == PLACES + item, ranks[other], codes)
        codes = codes.astype(F32).astype(BF)
        lanes = pl.ds(h * HS, HS)
        source = jnp.concatenate(
            [proj_ref[0, :, lanes], proj_ref[1, :, lanes], cot_ref[:, lanes]], axis=1
        )
        out_ref[:, pl.ds(h * 3 * HS, 3 * HS)] = dot(hot, source).astype(BF)
        marks += dot(hot, codes, 1, 1)
    out_ref[:, pl.ds(HH * 3 * HS, 128)] = marks.astype(BF)


def dispatch(odd, buckets, proj, cot):
    vmem = pl.BlockSpec(memory_space=pltpu.VMEM)
    return pl.pallas_call(
        dispatch_kernel,
        out_shape=(
            jax.ShapeDtypeStruct((ITEMS, TT), jnp.int32),
            jax.ShapeDtypeStruct((ROWS, WIRE), BF),
        ),
        in_specs=[pl.BlockSpec(memory_space=pltpu.SMEM), vmem, vmem, vmem],
        compiler_params=pltpu.CompilerParams(vmem_limit_bytes=VMEM),
        name="dispatch",
    )(odd, buckets, proj, cot)


def split_rounds(x):
    width = x.shape[1]
    x = x.reshape(NO, 3, 8, width)
    mixed = x[:, 1].reshape(NO // 2, 2, 8, width)
    even, odd = mixed[:, 0], mixed[:, 1]
    top = iota((NO // 2, 8, width), 1) < 4
    late0 = jnp.where(top, even, odd).reshape(SLOTS - MAIN, width)
    late1 = jnp.where(top, odd, even).reshape(SLOTS - MAIN, width)
    return (
        jnp.concatenate([x[:, 0].reshape(MAIN, width), late0], axis=0),
        jnp.concatenate([x[:, 2].reshape(MAIN, width), late1], axis=0),
    )


def join_rounds(x0, x1):
    width = x0.shape[1]
    late0 = x0[MAIN:].reshape(NO // 2, 8, width)
    late1 = x1[MAIN:].reshape(NO // 2, 8, width)
    top = iota((NO // 2, 8, width), 1) < 4
    even = jnp.where(top, late0, late1)
    odd = jnp.where(top, late1, late0)
    mixed = jnp.stack([even, odd], axis=1).reshape(NO, 1, 8, width)
    main0 = x0[:MAIN].reshape(NO, 1, 8, width)
    main1 = x1[:MAIN].reshape(NO, 1, 8, width)
    return jnp.concatenate([main0, mixed, main1], axis=1).reshape(ROWS, width)


def source_and_slot(shape, axis, which):
    row = iota(shape, axis)
    late = row - MAIN
    flip = ((late & 7) >= 4).astype(jnp.int32)
    source_late = 2 * lax.shift_right_arithmetic(late, 3) + (flip if which == 0 else 1 - flip)
    source = jnp.where(row < MAIN, lax.shift_right_logical(row, 3), source_late)
    slot = jnp.where(row < MAIN, row & 7, 8 + (late & 3))
    return source, slot


def forward_kernel(
    x_ref,
    probs_ref,
    rows_ref,
    self_ref,
    wire_ref,
    mine_ref,
    probs,
    rows,
    kept_all,
    wire,
    mine,
    bias,
    spread,
    far,
    sems,
):
    lane = iota((SLOTS, HS), 1)
    for r in range(RR):
        source_i, slot_i = source_and_slot((SLOTS, 1), 0, r)
        source_j, slot_j = source_and_slot((1, SLOTS), 1, r)
        earlier = source_j * CAP + slot_j < source_i * CAP + slot_i
        bias[r] = jnp.where(earlier, 0.0, FAR)
    for r, marks in enumerate(split_rounds(x_ref[:, pl.ds(3 * HH * HS, HS)].astype(F32))):
        held = (lane >= OWNERS) & (lane < CODES) & ((lane & 7) >> 2 == r)
        spread[r] = jnp.where(held, marks, 0.0)
        group = lane & (HS - 8)
        wanted = jnp.where(group == CODES, 1.0, jnp.where(group == CODES + 8, 2.0, 0.0))
        coded = (group >= CODES) & (group < CODES + 24)
        far[r, :, :HS] = jnp.where(coded & (marks == wanted), FAR, 0.0).astype(BF)
        other = coded & ((marks != wanted) | (group == CODES + 16))
        far[r, :, HS:] = jnp.where(other, 1.0, 0.0).astype(BF)

    copies = []
    for h in range(HH):
        rounds = split_rounds(x_ref[:, pl.ds(h * 3 * HS, 3 * HS)].astype(F32))
        for r in range(RR):
            x = rounds[r].astype(BF)
            q = rounds[r][:, :HS]
            u = rounds[r][:, 2 * HS :]
            v_half = x[:, HS : 2 * HS]
            scale = lax.rsqrt(jnp.sum(q * q, axis=1, keepdims=True) + 1e-06)
            unit = (q * scale).astype(BF)
            far_q = far[r, :, :HS] * ((lane & 7) == r * HH + h).astype(BF)
            far_k = far[r, :, HS:]
            scores = dot(
                jnp.concatenate([x[:, :HS], far_q], axis=1),
                jnp.concatenate([unit, far_k], axis=1),
                1,
                1,
            )
            scores = scores + bias[r]
            top = jnp.maximum(jnp.max(scores, axis=1, keepdims=True), SELF_SCORE / SCALE)
            shifted = jnp.exp2((scores - top) * POWER).astype(BF)
            own = jnp.exp2((SELF_SCORE / SCALE - top) * POWER)
            both = dot(shifted, jnp.concatenate([v_half, jnp.ones_like(v_half)], axis=1))
            totals = both[:, HS:] + own
            inverse = 1.0 / totals
            own = (own * inverse).astype(BF).astype(F32)
            out = both[:, :HS] * inverse + own * rounds[r][:, HS : 2 * HS]
            out = out.astype(BF).astype(F32)
            inner = jnp.sum(u * out, axis=1, keepdims=True)
            lse = top * SCALE + jnp.log(totals)
            probs[h, r] = shifted
            rows[h, r] = x
            kept = 0.0
            for at, column in enumerate((own, inner, scale, inverse)):
                kept = jnp.where(lane == at, column.astype(F32), kept)
            kept_all[h, r] = kept
            at = lane - (r * HH + h) * 2
            sent = jnp.where(at == 0, lse - LSE_SHIFT, spread[r])
            spread[r] = jnp.where(at == 1, inner, sent)
        for at, (here, there) in enumerate(
            ((probs, probs_ref), (rows, rows_ref), (kept_all, self_ref))
        ):
            copies.append(
                pltpu.make_async_copy(here.at[h], there.at[h], sems.at[3 * h + at])
            )
            copies[-1].start()

    total = jnp.zeros((HS, SLOTS), F32)
    for r in range(RR):
        source, slot = source_and_slot((SLOTS, 1), 0, r)
        hot = (iota((SLOTS, SLOTS), 1) == slot * NO + source).astype(BF)
        total += dot(spread[r].astype(BF), hot, 0, 0)
    total = total.astype(BF)
    mine[...] = total
    total = total[: 2 * ITEMS]
    for k in range(NO):
        wire[pl.ds(k * 2 * ITEMS, 2 * ITEMS), :] = total
    copies += [
        pltpu.make_async_copy(mine, mine_ref, sems.at[3 * HH]),
        pltpu.make_async_copy(wire, wire_ref, sems.at[3 * HH + 1]),
    ]
    copies[-1].start()
    copies[-2].start()
    for copy in copies:
        copy.wait()


def forward(received):
    shapes = (
        ((HH, RR, SLOTS, SLOTS), BF),
        ((HH, RR, SLOTS, 3 * HS), BF),
        ((HH, RR, SLOTS, HS), F32),
        ((NO * 2 * ITEMS, SLOTS), BF),
        ((HS, SLOTS), BF),
    )
    return pl.pallas_call(
        forward_kernel,
        out_shape=tuple(pltpu.HBM(*shape) for shape in shapes),
        in_specs=[pl.BlockSpec(memory_space=pltpu.VMEM)],
        out_specs=(pl.BlockSpec(memory_space=pl.ANY),) * len(shapes),
        scratch_shapes=[pltpu.VMEM(*shape) for shape in shapes]
        + [
            pltpu.VMEM((RR, SLOTS, SLOTS), F32),
            pltpu.VMEM((RR, SLOTS, HS), F32),
            pltpu.VMEM((RR, SLOTS, 2 * HS), BF),
            pltpu.SemaphoreType.DMA((3 * HH + 2,)),
        ],
        compiler_params=pltpu.CompilerParams(vmem_limit_bytes=VMEM),
        name="forward",
    )(received)


def between_kernel(probs_ref, rows_ref, self_ref, probs_t_ref, weighted_t_ref, sums_ref):
    for r in range(RR):
        probs = (probs_ref[0, r].astype(F32) * self_ref[0, r, :, 3:4]).astype(BF)
        q = rows_ref[0, r, :, :HS]
        v = rows_ref[0, r, :, HS : 2 * HS]
        u = rows_ref[0, r, :, 2 * HS :]
        inner = self_ref[0, r, :, 1:2]
        scale = self_ref[0, r, :, 2:3]
        unit = (q.astype(F32) * scale).astype(BF)
        weighted = (probs.astype(F32) * (dot(u, v, 1, 1) - inner)).astype(BF)
        probs_t_ref[0, r] = probs.T
        weighted_t_ref[0, r] = weighted.T
        sums_ref[0, r, :, :HS] = dot(weighted, unit).astype(BF)
        sums_ref[0, r, :, HS : 2 * HS] = dot(probs, unit).astype(BF)
        own = self_ref[0, r, :, 0:1]
        sums_ref[0, r, :, 2 * HS :] = jnp.broadcast_to(own, (SLOTS, HS)).astype(BF)


SQUARE = pl.BlockSpec((1, RR, SLOTS, SLOTS), lambda h: (h, 0, 0, 0))
NARROW = pl.BlockSpec((1, RR, SLOTS, HS), lambda h: (h, 0, 0, 0))
WIDE = pl.BlockSpec((1, RR, SLOTS, 3 * HS), lambda h: (h, 0, 0, 0))


def between(probs, rows, own):
    flops = ITEMS * SLOTS * SLOTS * HS * 6
    return pl.pallas_call(
        between_kernel,
        grid=(HH,),
        out_shape=(
            pltpu.HBM((HH, RR, SLOTS, SLOTS), BF),
            pltpu.HBM((HH, RR, SLOTS, SLOTS), BF),
            pltpu.HBM((HH, RR, SLOTS, 3 * HS), BF),
        ),
        in_specs=[SQUARE, WIDE, NARROW],
        out_specs=(SQUARE, SQUARE, WIDE),
        compiler_params=pltpu.CompilerParams(vmem_limit_bytes=VMEM),
        cost_estimate=pl.CostEstimate(flops=flops, bytes_accessed=12 << 20, transcendentals=0),
        name="between",
    )(pinned(probs), pinned(rows), pinned(own))


def round_shares(mine_ref, got_ref, got, put):
    for at in range(SLOTS // HS):
        got[at, : NO * 2 * ITEMS] = got_ref[:, pl.ds(at * HS, HS)].astype(F32)
    mine = mine_ref[...].astype(F32)
    owner_ids = iota((3 * NO, SLOTS), 0)
    slot_ids = iota((HS, SLOTS), 0)
    source = iota((1, SLOTS), 1) & (NO - 1)
    mine_lse, mine_inner, other_lse, other_inner = [], [], [], []
    for item in range(ITEMS):
        first_row = (item ^ HH) * 2
        table = jnp.concatenate(
            [
                jnp.concatenate(
                    [
                        got[i, pl.ds(first_row + at, NO, stride=2 * ITEMS), :]
                        for i in range(SLOTS // HS)
                    ],
                    axis=0,
                ).astype(BF)
                for at in range(2)
            ],
            axis=1,
        )
        owner = mine[OWNERS + item : OWNERS + item + 1].astype(jnp.int32)
        slot = mine[PLACES + item : PLACES + item + 1].astype(jnp.int32)
        hot = (owner_ids == lax.shift_right_logical(slot, 2) * NO + owner).astype(BF)
        here = slot_ids == (slot & 3) * NO + source
        seen = dot(table, hot, 0, 0)
        other_lse.append(jnp.sum(jnp.where(here, seen[:HS], 0.0), axis=0, keepdims=True))
        other_inner.append(jnp.sum(jnp.where(here, seen[HS:], 0.0), axis=0, keepdims=True))
        mine_lse.append(mine[item * 2 : item * 2 + 1])
        mine_inner.append(mine[item * 2 + 1 : item * 2 + 2])
    mine_lse, mine_inner, other_lse, other_inner = (
        jnp.concatenate(x, axis=0) for x in (mine_lse, mine_inner, other_lse, other_inner)
    )
    top = jnp.maximum(mine_lse, other_lse)
    share = jnp.exp(mine_lse - top)
    other_share = jnp.exp(other_lse - top)
    inverse = 1.0 / (share + other_share)
    share = share * inverse
    shift = other_share * inverse * (other_inner - mine_inner)
    high, low = halves(jnp.concatenate([share, shift], axis=0))
    both = jnp.concatenate([high, low], axis=1)
    for r in range(RR):
        source, slot = source_and_slot((SLOTS, 1), 0, r)
        hot = (iota((SLOTS, SLOTS), 1) == slot * NO + source).astype(BF)
        columns = dot(jnp.concatenate([hot, hot], axis=1), both, 1, 1)
        for h in range(HH):
            item = r * HH + h
            put[h, r, :, :HS] = jnp.broadcast_to(columns[:, item : item + 1], (SLOTS, HS))
            item += ITEMS
            put[h, r, :, HS:] = jnp.broadcast_to(columns[:, item : item + 1], (SLOTS, HS))


def backward_kernel(
    probs_ref,
    weighted_ref,
    rows_ref,
    sums_ref,
    mine_ref,
    got_ref,
    out_ref,
    probs,
    weighted,
    queries,
    upstream,
    sums,
    out,
    got,
    put,
    sems,
):
    loads = []
    for h in range(HH):
        pairs = (
            (probs_ref.at[h], probs.at[h]),
            (weighted_ref.at[h], weighted.at[h]),
            (rows_ref.at[h, :, :, pl.ds(0, HS)], queries.at[h]),
            (rows_ref.at[h, :, :, pl.ds(2 * HS, HS)], upstream.at[h]),
            (sums_ref.at[h], sums.at[h]),
        )
        loads.append(
            [pltpu.make_async_copy(*p, sems.at[6 * h + at]) for at, p in enumerate(pairs)]
        )
        for copy in loads[h]:
            copy.start()
    round_shares(mine_ref, got_ref, got, put)
    stores = []
    for h in range(HH):
        for copy in loads[h]:
            copy.wait()
        grads = []
        for r in range(RR):
            share = put[h, r, :, :HS]
            shift = put[h, r, :, HS:]
            q = queries[h, r].astype(F32)
            u_share = share * upstream[h, r].astype(F32)
            q_share = share * q
            right = jnp.concatenate([-shift * q_share, u_share], axis=1).astype(BF)
            both = dot(probs[h, r], right)
            unit_grad = (dot(weighted[h, r], q_share.astype(BF)) + both[:, :HS]) * SCALE
            value_grad = both[:, HS:] + sums[h, r, :, 2 * HS :].astype(F32) * u_share
            scale = lax.rsqrt(jnp.sum(q * q, axis=1, keepdims=True) + 1e-06)
            along = jnp.sum(q * unit_grad, axis=1, keepdims=True)
            first = sums[h, r, :, :HS].astype(F32)
            second = sums[h, r, :, HS : 2 * HS].astype(F32)
            query_grad = (share * SCALE) * (first - shift * second)
            query_grad += scale * unit_grad - q * (scale * scale * scale * along)
            grads.append(jnp.concatenate([query_grad, value_grad], axis=1))
        out[h] = join_rounds(grads[0], grads[1]).astype(BF)
        there = out_ref.at[:, pl.ds(h * 2 * HS, 2 * HS)]
        stores.append(pltpu.make_async_copy(out.at[h], there, sems.at[6 * h + 5]))
        stores[h].start()
    for copy in stores:
        copy.wait()


def pinned(x):
    return pltpu.with_memory_space_constraint(x, pltpu.HBM)


def backward(probs, weighted, rows, sums, mine, got):
    hbm = pl.BlockSpec(memory_space=pl.ANY)
    vmem = pl.BlockSpec(memory_space=pltpu.VMEM)
    return pl.pallas_call(
        backward_kernel,
        out_shape=pltpu.HBM((ROWS, HH * 2 * HS), BF),
        in_specs=[hbm, hbm, hbm, hbm, vmem, vmem],
        out_specs=hbm,
        scratch_shapes=[
            pltpu.VMEM((HH, RR, SLOTS, SLOTS), BF),
            pltpu.VMEM((HH, RR, SLOTS, SLOTS), BF),
            pltpu.VMEM((HH, RR, SLOTS, HS), BF),
            pltpu.VMEM((HH, RR, SLOTS, HS), BF),
            pltpu.VMEM((HH, RR, SLOTS, 3 * HS), BF),
            pltpu.VMEM((HH, ROWS, 2 * HS), BF),
            pltpu.VMEM((SLOTS // HS, (NO + 1) * 2 * ITEMS, HS), F32),
            pltpu.VMEM((HH, RR, SLOTS, 2 * HS), F32),
            pltpu.SemaphoreType.DMA((6 * HH,)),
        ],
        compiler_params=pltpu.CompilerParams(vmem_limit_bytes=VMEM),
        name="backward",
    )(pinned(probs), pinned(weighted), pinned(rows), pinned(sums), mine, got)


def collect_kernel(rows_ref, got_ref, out_ref):
    row_ids = iota((TT, ROWS), 1)
    for h in range(HH):
        first = row_ids == rows_ref[:, h : h + 1]
        second = row_ids == rows_ref[:, HH + h : HH + h + 1]
        hot = (first | second).astype(BF)
        sums = dot(hot, got_ref[:, pl.ds(h * 2 * HS, 2 * HS)]).astype(BF)
        out_ref[0, :, pl.ds(h * HS, HS)] = sums[:, :HS]
        out_ref[1, :, pl.ds(h * HS, HS)] = sums[:, HS:]


def collect(rows, got):
    vmem = pl.BlockSpec(memory_space=pltpu.VMEM)
    return pl.pallas_call(
        collect_kernel,
        out_shape=jax.ShapeDtypeStruct((2, TT, HH * HS), BF),
        in_specs=[vmem, vmem],
        out_specs=vmem,
        compiler_params=pltpu.CompilerParams(vmem_limit_bytes=12 * 1024 * 1024),
        name="collect",
    )(rows, got)


def exchange(x):
    return lax.all_to_all(x, "seq", split_axis=0, concat_axis=0, tiled=True)


def block_order(me):
    return [me, me ^ 3, me ^ 1, me ^ 2]


def blocks_of(x, me):
    size = x.shape[1] // 4
    parts = [lax.dynamic_slice_in_dim(x, i * size, size, 1) for i in block_order(me)]
    return jnp.concatenate(parts, axis=1)


def swap(x, mask):
    return lax.ppermute(x, "bkt", [(i, i ^ mask) for i in range(4)])


PARTS = 4


def per_device(tokens, weights, cotangent, buckets):
    odd = (lax.axis_index("seq") & 1).astype(jnp.int32).reshape(1)
    me = lax.axis_index("bkt")
    projected = jnp.einsum(
        "td,dcf->ctf", tokens, weights, preferred_element_type=jnp.float32
    ).astype(jnp.bfloat16)
    rows, send = dispatch(odd, buckets, projected, cotangent)
    received = exchange(send)
    rows = blocks_of(rows, me).T
    probs, held, own, wire, mine = forward(received)
    everyones = exchange(wire)
    probs_t, weighted_t, sums = between(probs, held, own)
    slot_grads = exchange(backward(probs_t, weighted_t, held, sums, mine, everyones))
    grads = collect(rows, slot_grads)
    width = weights.shape[0] // PARTS
    slabs = lax.optimization_barrier(
        [weights[i * width : (i + 1) * width].transpose(1, 0, 2) for i in range(PARTS)]
    )
    sums = []
    for i, slab in enumerate(slabs):
        part = jnp.einsum("ctf,cdf->td", grads, slab, preferred_element_type=jnp.float32)
        part = part.astype(jnp.bfloat16).reshape(4, TT // 4, width)
        if i % 2 == 0:
            sums.append(part[:2] + swap(part[2:], 1))
        else:
            sums.append(
                jnp.stack([part[0], part[2]]) + swap(jnp.stack([part[1], part[3]]), 3)
            )
    outs = [x[0] + swap(x[1], 3 if i % 2 == 0 else 1) for i, x in enumerate(sums)]
    return jnp.concatenate(outs, axis=1)


def solution(mesh):
    in_specs = (P("seq", None), P(None, None, "bkt"), P("seq", "bkt"), P(None, "bkt", "seq"))
    out_specs = P(("seq", "bkt"), None)
    return jax.shard_map(
        per_device, mesh=mesh, in_specs=in_specs, out_specs=out_specs, check_vma=False
    )
```

```python
import functools
import math

import jax
import jax.numpy as jnp
from jax import lax
from jax.experimental import pallas as pl
from jax.experimental.pallas import tpu as pltpu
from jax.sharding import PartitionSpec as P

HH = 4
RR = 2
TT = 256
HS = 128
NO = 32
CAP = 12
ROWS = NO * 24
SLOTS = NO * CAP
MAIN = NO * 8
ITEMS = HH * RR
SCALE = 1.0 / math.sqrt(HS)
POWER = SCALE / math.log(2.0)
SELF_SCORE = -100000.0
FAR = -(2.0**30)
LSE_SHIFT = 4.5
F32 = jnp.float32
BF = jnp.bfloat16
VMEM = 24 * 1024 * 1024


def iota(shape, axis):
    return lax.broadcasted_iota(jnp.int32, shape, axis)


def dot(a, b, ca=1, cb=0, precision=None):
    return lax.dot_general(
        a, b, (((ca,), (cb,)), ((), ())), preferred_element_type=F32, precision=precision
    )


def halves(x):
    high = x.astype(BF)
    return high, (x - high.astype(F32)).astype(BF)


WIRE = HH * 3 * HS + 128
OWNERS = 32
PLACES = 40
CODES = 64


def dispatch_kernel(odd_ref, buckets_ref, proj_ref, cot_ref, rows_ref, out_ref):
    odd = odd_ref[0]
    before = (iota((TT, TT), 0) < iota((TT, TT), 1)).astype(BF)
    owner_ids = iota((NO, TT), 0)
    row_ids = iota((ROWS, TT), 0)
    buckets = [buckets_ref[r, h : h + 1, :] for r in range(RR) for h in range(HH)]
    hots = [owner_ids == lax.shift_right_logical(mine, 1) for mine in buckets]
    counts = dot(jnp.concatenate([hot.astype(BF) for hot in hots], axis=0), before)
    rows, ranks = [], []
    for item in range(ITEMS):
        count = counts[item * NO : (item + 1) * NO]
        rank = jnp.sum(jnp.where(hots[item], count, 0.0), axis=0, keepdims=True)
        rank = rank.astype(jnp.int32)
        first = item // HH
        late = 4 * odd if first == 0 else 4 - 4 * odd
        row = jnp.where(rank < 8, rank + 16 * first, rank + late)
        rows.append(lax.shift_right_logical(buckets[item], 1) * 24 + row)
        ranks.append(rank)
        rows_ref[item : item + 1, :] = rows[item]
    code_ids = iota((128, TT), 0)
    marks = jnp.zeros((ROWS, 128), F32)
    for h in range(HH):
        hot = ((row_ids == rows[h]) | (row_ids == rows[HH + h])).astype(BF)
        codes = 0
        for item, other in ((h, HH + h), (HH + h, h)):
            bucket = 1 + (buckets[item] & 1)
            codes = jnp.where((code_ids >= CODES) & (code_ids & 7 == item), bucket, codes)
            owner = lax.shift_right_logical(buckets[other], 1)
            codes = jnp.where(code_ids == OWNERS + item, owner, codes)
            codes = jnp.where(code_ids == PLACES + item, ranks[other], codes)
        codes = codes.astype(F32).astype(BF)
        lanes = pl.ds(h * HS, HS)
        source = jnp.concatenate(
            [proj_ref[0, :, lanes], proj_ref[1, :, lanes], cot_ref[:, lanes]], axis=1
        )
        out_ref[:, pl.ds(h * 3 * HS, 3 * HS)] = dot(hot, source).astype(BF)
        marks += dot(hot, codes, 1, 1)
    out_ref[:, pl.ds(HH * 3 * HS, 128)] = marks.astype(BF)


def dispatch(odd, buckets, proj, cot):
    vmem = pl.BlockSpec(memory_space=pltpu.VMEM)
    return pl.pallas_call(
        dispatch_kernel,
        out_shape=(
            jax.ShapeDtypeStruct((ITEMS, TT), jnp.int32),
            jax.ShapeDtypeStruct((ROWS, WIRE), BF),
        ),
        in_specs=[pl.BlockSpec(memory_space=pltpu.SMEM), vmem, vmem, vmem],
        compiler_params=pltpu.CompilerParams(vmem_limit_bytes=VMEM),
        name="dispatch",
    )(odd, buckets, proj, cot)


def split_rounds(x):
    width = x.shape[1]
    x = x.reshape(NO, 3, 8, width)
    mixed = x[:, 1].reshape(NO // 2, 2, 8, width)
    even, odd = mixed[:, 0], mixed[:, 1]
    top = iota((NO // 2, 8, width), 1) < 4
    late0 = jnp.where(top, even, odd).reshape(SLOTS - MAIN, width)
    late1 = jnp.where(top, odd, even).reshape(SLOTS - MAIN, width)
    return (
        jnp.concatenate([x[:, 0].reshape(MAIN, width), late0], axis=0),
        jnp.concatenate([x[:, 2].reshape(MAIN, width), late1], axis=0),
    )


def join_rounds(x0, x1):
    width = x0.shape[1]
    late0 = x0[MAIN:].reshape(NO // 2, 8, width)
    late1 = x1[MAIN:].reshape(NO // 2, 8, width)
    top = iota((NO // 2, 8, width), 1) < 4
    even = jnp.where(top, late0, late1)
    odd = jnp.where(top, late1, late0)
    mixed = jnp.stack([even, odd], axis=1).reshape(NO, 1, 8, width)
    main0 = x0[:MAIN].reshape(NO, 1, 8, width)
    main1 = x1[:MAIN].reshape(NO, 1, 8, width)
    return jnp.concatenate([main0, mixed, main1], axis=1).reshape(ROWS, width)


def source_and_slot(shape, axis, which):
    row = iota(shape, axis)
    late = row - MAIN
    flip = ((late & 7) >= 4).astype(jnp.int32)
    source_late = 2 * lax.shift_right_arithmetic(late, 3) + (flip if which == 0 else 1 - flip)
    source = jnp.where(row < MAIN, lax.shift_right_logical(row, 3), source_late)
    slot = jnp.where(row < MAIN, row & 7, 8 + (late & 3))
    return source, slot


def forward_kernel(
    x_ref,
    probs_ref,
    rows_ref,
    self_ref,
    wire_ref,
    mine_ref,
    probs,
    rows,
    kept_all,
    wire,
    mine,
    bias,
    spread,
    far,
    sems,
):
    lane = iota((SLOTS, HS), 1)
    for r in range(RR):
        source_i, slot_i = source_and_slot((SLOTS, 1), 0, r)
        source_j, slot_j = source_and_slot((1, SLOTS), 1, r)
        earlier = source_j * CAP + slot_j < source_i * CAP + slot_i
        bias[r] = jnp.where(earlier, 0.0, FAR)
    for r, marks in enumerate(split_rounds(x_ref[:, pl.ds(3 * HH * HS, HS)].astype(F32))):
        held = (lane >= OWNERS) & (lane < CODES) & ((lane & 7) >> 2 == r)
        spread[r] = jnp.where(held, marks, 0.0)
        group = lane & (HS - 8)
        wanted = jnp.where(group == CODES, 1.0, jnp.where(group == CODES + 8, 2.0, 0.0))
        coded = (group >= CODES) & (group < CODES + 24)
        far[r, :, :HS] = jnp.where(coded & (marks == wanted), FAR, 0.0).astype(BF)
        other = coded & ((marks != wanted) | (group == CODES + 16))
        far[r, :, HS:] = jnp.where(other, 1.0, 0.0).astype(BF)

    copies = []

    def send(here, there):
        copies.append(pltpu.make_async_copy(here, there, sems.at[len(copies)]))
        copies[-1].start()

    for h in range(HH):
        rounds = split_rounds(x_ref[:, pl.ds(h * 3 * HS, 3 * HS)].astype(F32))
        for r in range(RR):
            x = rounds[r].astype(BF)
            rows[h, r] = x
            send(rows.at[h, r], rows_ref.at[h, r])
            q = rounds[r][:, :HS]
            u = rounds[r][:, 2 * HS :]
            v_half = x[:, HS : 2 * HS]
            scale = lax.rsqrt(jnp.sum(q * q, axis=1, keepdims=True) + 1e-06)
            unit = (q * scale).astype(BF)
            far_q = far[r, :, :HS] * ((lane & 7) == r * HH + h).astype(BF)
            far_k = far[r, :, HS:]
            scores = dot(
                jnp.concatenate([x[:, :HS], far_q], axis=1),
                jnp.concatenate([unit, far_k], axis=1),
                1,
                1,
            )
            scores = scores + bias[r]
            top = jnp.maximum(jnp.max(scores, axis=1, keepdims=True), SELF_SCORE / SCALE)
            shifted = jnp.exp2((scores - top) * POWER).astype(BF)
            probs[h, r] = shifted
            send(probs.at[h, r], probs_ref.at[h, r])
            own = jnp.exp2((SELF_SCORE / SCALE - top) * POWER)
            both = dot(shifted, jnp.concatenate([v_half, jnp.ones_like(v_half)], axis=1))
            totals = both[:, HS:] + own
            inverse = 1.0 / totals
            own = (own * inverse).astype(BF).astype(F32)
            out = both[:, :HS] * inverse + own * rounds[r][:, HS : 2 * HS]
            out = out.astype(BF).astype(F32)
            inner = jnp.sum(u * out, axis=1, keepdims=True)
            lse = top * SCALE + jnp.log(totals)
            kept = 0.0
            for at, column in enumerate((own, inner, scale, inverse)):
                kept = jnp.where(lane == at, column.astype(F32), kept)
            kept_all[h, r] = kept
            send(kept_all.at[h, r], self_ref.at[h, r])
            at = lane - (r * HH + h) * 2
            sent = jnp.where(at == 0, lse - LSE_SHIFT, spread[r])
            spread[r] = jnp.where(at == 1, inner, sent)

    total = jnp.zeros((HS, SLOTS), F32)
    for r in range(RR):
        source, slot = source_and_slot((SLOTS, 1), 0, r)
        hot = (iota((SLOTS, SLOTS), 1) == slot * NO + source).astype(BF)
        total += dot(spread[r].astype(BF), hot, 0, 0)
    total = total.astype(BF)
    mine[...] = total
    total = total[: 2 * ITEMS]
    for k in range(NO):
        wire[pl.ds(k * 2 * ITEMS, 2 * ITEMS), :] = total
    send(wire, wire_ref)
    send(mine, mine_ref)
    for copy in copies:
        copy.wait()


def forward(received):
    shapes = (
        ((HH, RR, SLOTS, SLOTS), BF),
        ((HH, RR, SLOTS, 3 * HS), BF),
        ((HH, RR, SLOTS, HS), F32),
        ((NO * 2 * ITEMS, SLOTS), BF),
        ((HS, SLOTS), BF),
    )
    return pl.pallas_call(
        forward_kernel,
        out_shape=tuple(pltpu.HBM(*shape) for shape in shapes),
        in_specs=[pl.BlockSpec(memory_space=pltpu.VMEM)],
        out_specs=(pl.BlockSpec(memory_space=pl.ANY),) * len(shapes),
        scratch_shapes=[pltpu.VMEM(*shape) for shape in shapes]
        + [
            pltpu.VMEM((RR, SLOTS, SLOTS), F32),
            pltpu.VMEM((RR, SLOTS, HS), F32),
            pltpu.VMEM((RR, SLOTS, 2 * HS), BF),
            pltpu.SemaphoreType.DMA((3 * ITEMS + 2,)),
        ],
        compiler_params=pltpu.CompilerParams(vmem_limit_bytes=VMEM),
        name="forward",
    )(received)


def between_kernel(probs_ref, rows_ref, self_ref, probs_t_ref, weighted_t_ref, sums_ref):
    for r in range(RR):
        probs = (probs_ref[0, r].astype(F32) * self_ref[0, r, :, 3:4]).astype(BF)
        q = rows_ref[0, r, :, :HS]
        v = rows_ref[0, r, :, HS : 2 * HS]
        u = rows_ref[0, r, :, 2 * HS :]
        inner = self_ref[0, r, :, 1:2]
        scale = self_ref[0, r, :, 2:3]
        unit = (q.astype(F32) * scale).astype(BF)
        weighted = (probs.astype(F32) * (dot(u, v, 1, 1) - inner)).astype(BF)
        probs_t_ref[0, r] = probs.T
        weighted_t_ref[0, r] = weighted.T
        sums_ref[0, r, :, :HS] = dot(weighted, unit).astype(BF)
        sums_ref[0, r, :, HS : 2 * HS] = dot(probs, unit).astype(BF)
        own = self_ref[0, r, :, 0:1]
        sums_ref[0, r, :, 2 * HS :] = jnp.broadcast_to(own, (SLOTS, HS)).astype(BF)


SQUARE = pl.BlockSpec((1, RR, SLOTS, SLOTS), lambda h: (h, 0, 0, 0))
NARROW = pl.BlockSpec((1, RR, SLOTS, HS), lambda h: (h, 0, 0, 0))
WIDE = pl.BlockSpec((1, RR, SLOTS, 3 * HS), lambda h: (h, 0, 0, 0))


def between(probs, rows, own):
    flops = ITEMS * SLOTS * SLOTS * HS * 6
    return pl.pallas_call(
        between_kernel,
        grid=(HH,),
        out_shape=(
            pltpu.HBM((HH, RR, SLOTS, SLOTS), BF),
            pltpu.HBM((HH, RR, SLOTS, SLOTS), BF),
            pltpu.HBM((HH, RR, SLOTS, 3 * HS), BF),
        ),
        in_specs=[SQUARE, WIDE, NARROW],
        out_specs=(SQUARE, SQUARE, WIDE),
        compiler_params=pltpu.CompilerParams(vmem_limit_bytes=VMEM),
        cost_estimate=pl.CostEstimate(flops=flops, bytes_accessed=12 << 20, transcendentals=0),
        name="between",
    )(pinned(probs), pinned(rows), pinned(own))


def round_shares(mine_ref, got_ref, got, put):
    for at in range(SLOTS // HS):
        got[at, : NO * 2 * ITEMS] = got_ref[:, pl.ds(at * HS, HS)].astype(F32)
    mine = mine_ref[...].astype(F32)
    owner_ids = iota((3 * NO, SLOTS), 0)
    slot_ids = iota((HS, SLOTS), 0)
    source = iota((1, SLOTS), 1) & (NO - 1)
    mine_lse, mine_inner, other_lse, other_inner = [], [], [], []
    for item in range(ITEMS):
        first_row = (item ^ HH) * 2
        table = jnp.concatenate(
            [
                jnp.concatenate(
                    [
                        got[i, pl.ds(first_row + at, NO, stride=2 * ITEMS), :]
                        for i in range(SLOTS // HS)
                    ],
                    axis=0,
                ).astype(BF)
                for at in range(2)
            ],
            axis=1,
        )
        owner = mine[OWNERS + item : OWNERS + item + 1].astype(jnp.int32)
        slot = mine[PLACES + item : PLACES + item + 1].astype(jnp.int32)
        hot = (owner_ids == lax.shift_right_logical(slot, 2) * NO + owner).astype(BF)
        here = slot_ids == (slot & 3) * NO + source
        seen = dot(table, hot, 0, 0)
        other_lse.append(jnp.sum(jnp.where(here, seen[:HS], 0.0), axis=0, keepdims=True))
        other_inner.append(jnp.sum(jnp.where(here, seen[HS:], 0.0), axis=0, keepdims=True))
        mine_lse.append(mine[item * 2 : item * 2 + 1])
        mine_inner.append(mine[item * 2 + 1 : item * 2 + 2])
    mine_lse, mine_inner, other_lse, other_inner = (
        jnp.concatenate(x, axis=0) for x in (mine_lse, mine_inner, other_lse, other_inner)
    )
    top = jnp.maximum(mine_lse, other_lse)
    share = jnp.exp(mine_lse - top)
    other_share = jnp.exp(other_lse - top)
    inverse = 1.0 / (share + other_share)
    share = share * inverse
    shift = other_share * inverse * (other_inner - mine_inner)
    high, low = halves(jnp.concatenate([share, shift], axis=0))
    both = jnp.concatenate([high, low], axis=1)
    for r in range(RR):
        source, slot = source_and_slot((SLOTS, 1), 0, r)
        hot = (iota((SLOTS, SLOTS), 1) == slot * NO + source).astype(BF)
        columns = dot(jnp.concatenate([hot, hot], axis=1), both, 1, 1)
        for h in range(HH):
            item = r * HH + h
            put[h, r, :, :HS] = jnp.broadcast_to(columns[:, item : item + 1], (SLOTS, HS))
            item += ITEMS
            put[h, r, :, HS:] = jnp.broadcast_to(columns[:, item : item + 1], (SLOTS, HS))


def backward_kernel(
    probs_ref,
    weighted_ref,
    rows_ref,
    sums_ref,
    mine_ref,
    got_ref,
    out_ref,
    probs,
    weighted,
    queries,
    upstream,
    sums,
    out,
    got,
    put,
    sems,
):
    loads = []
    for h in range(HH):
        pairs = (
            (probs_ref.at[h], probs.at[h]),
            (weighted_ref.at[h], weighted.at[h]),
            (rows_ref.at[h, :, :, pl.ds(0, HS)], queries.at[h]),
            (rows_ref.at[h, :, :, pl.ds(2 * HS, HS)], upstream.at[h]),
            (sums_ref.at[h], sums.at[h]),
        )
        loads.append(
            [pltpu.make_async_copy(*p, sems.at[6 * h + at]) for at, p in enumerate(pairs)]
        )
        for copy in loads[h]:
            copy.start()
    round_shares(mine_ref, got_ref, got, put)
    stores = []
    for h in range(HH):
        for copy in loads[h]:
            copy.wait()
        grads = []
        for r in range(RR):
            share = put[h, r, :, :HS]
            shift = put[h, r, :, HS:]
            q = queries[h, r].astype(F32)
            u_share = share * upstream[h, r].astype(F32)
            q_share = share * q
            right = jnp.concatenate([-shift * q_share, u_share], axis=1).astype(BF)
            both = dot(probs[h, r], right)
            unit_grad = (dot(weighted[h, r], q_share.astype(BF)) + both[:, :HS]) * SCALE
            value_grad = both[:, HS:] + sums[h, r, :, 2 * HS :].astype(F32) * u_share
            scale = lax.rsqrt(jnp.sum(q * q, axis=1, keepdims=True) + 1e-06)
            along = jnp.sum(q * unit_grad, axis=1, keepdims=True)
            first = sums[h, r, :, :HS].astype(F32)
            second = sums[h, r, :, HS : 2 * HS].astype(F32)
            query_grad = (share * SCALE) * (first - shift * second)
            query_grad += scale * unit_grad - q * (scale * scale * scale * along)
            grads.append(jnp.concatenate([query_grad, value_grad], axis=1))
        out[h] = join_rounds(grads[0], grads[1]).astype(BF)
        there = out_ref.at[:, pl.ds(h * 2 * HS, 2 * HS)]
        stores.append(pltpu.make_async_copy(out.at[h], there, sems.at[6 * h + 5]))
        stores[h].start()
    for copy in stores:
        copy.wait()


def pinned(x):
    return pltpu.with_memory_space_constraint(x, pltpu.HBM)


def backward(probs, weighted, rows, sums, mine, got):
    hbm = pl.BlockSpec(memory_space=pl.ANY)
    vmem = pl.BlockSpec(memory_space=pltpu.VMEM)
    return pl.pallas_call(
        backward_kernel,
        out_shape=pltpu.HBM((ROWS, HH * 2 * HS), BF),
        in_specs=[hbm, hbm, hbm, hbm, vmem, vmem],
        out_specs=hbm,
        scratch_shapes=[
            pltpu.VMEM((HH, RR, SLOTS, SLOTS), BF),
            pltpu.VMEM((HH, RR, SLOTS, SLOTS), BF),
            pltpu.VMEM((HH, RR, SLOTS, HS), BF),
            pltpu.VMEM((HH, RR, SLOTS, HS), BF),
            pltpu.VMEM((HH, RR, SLOTS, 3 * HS), BF),
            pltpu.VMEM((HH, ROWS, 2 * HS), BF),
            pltpu.VMEM((SLOTS // HS, (NO + 1) * 2 * ITEMS, HS), F32),
            pltpu.VMEM((HH, RR, SLOTS, 2 * HS), F32),
            pltpu.SemaphoreType.DMA((6 * HH,)),
        ],
        compiler_params=pltpu.CompilerParams(vmem_limit_bytes=VMEM),
        name="backward",
    )(pinned(probs), pinned(weighted), pinned(rows), pinned(sums), mine, got)


def collect_kernel(rows_ref, got_ref, out_ref):
    row_ids = iota((TT, ROWS), 1)
    for h in range(HH):
        first = row_ids == rows_ref[:, h : h + 1]
        second = row_ids == rows_ref[:, HH + h : HH + h + 1]
        hot = (first | second).astype(BF)
        sums = dot(hot, got_ref[:, pl.ds(h * 2 * HS, 2 * HS)]).astype(BF)
        out_ref[0, :, pl.ds(h * HS, HS)] = sums[:, :HS]
        out_ref[1, :, pl.ds(h * HS, HS)] = sums[:, HS:]


def collect(rows, got):
    vmem = pl.BlockSpec(memory_space=pltpu.VMEM)
    return pl.pallas_call(
        collect_kernel,
        out_shape=jax.ShapeDtypeStruct((2, TT, HH * HS), BF),
        in_specs=[vmem, vmem],
        out_specs=vmem,
        compiler_params=pltpu.CompilerParams(vmem_limit_bytes=12 * 1024 * 1024),
        name="collect",
    )(rows, got)


def exchange(x):
    return lax.all_to_all(x, "seq", split_axis=0, concat_axis=0, tiled=True)


def block_order(me):
    return [me, me ^ 3, me ^ 1, me ^ 2]


def blocks_of(x, me):
    size = x.shape[1] // 4
    parts = [lax.dynamic_slice_in_dim(x, i * size, size, 1) for i in block_order(me)]
    return jnp.concatenate(parts, axis=1)


def swap(x, mask):
    return lax.ppermute(x, "bkt", [(i, i ^ mask) for i in range(4)])


PARTS = 4


def per_device(tokens, weights, cotangent, buckets):
    odd = (lax.axis_index("seq") & 1).astype(jnp.int32).reshape(1)
    me = lax.axis_index("bkt")
    projected = jnp.einsum(
        "td,dcf->ctf", tokens, weights, preferred_element_type=jnp.float32
    ).astype(jnp.bfloat16)
    rows, send = dispatch(odd, buckets, projected, cotangent)
    received = exchange(send)
    rows = blocks_of(rows, me).T
    probs, held, own, wire, mine = forward(received)
    everyones = exchange(wire)
    probs_t, weighted_t, sums = between(probs, held, own)
    slot_grads = exchange(backward(probs_t, weighted_t, held, sums, mine, everyones))
    grads = collect(rows, slot_grads)
    width = weights.shape[0] // PARTS
    slabs = lax.optimization_barrier(
        [weights[i * width : (i + 1) * width].transpose(1, 0, 2) for i in range(PARTS)]
    )
    sums = []
    for i, slab in enumerate(slabs):
        part = jnp.einsum("ctf,cdf->td", grads, slab, preferred_element_type=jnp.float32)
        part = part.astype(jnp.bfloat16).reshape(4, TT // 4, width)
        if i % 2 == 0:
            sums.append(part[:2] + swap(part[2:], 1))
        else:
            sums.append(
                jnp.stack([part[0], part[2]]) + swap(jnp.stack([part[1], part[3]]), 3)
            )
    outs = [x[0] + swap(x[1], 3 if i % 2 == 0 else 1) for i, x in enumerate(sums)]
    return jnp.concatenate(outs, axis=1)


def solution(mesh):
    in_specs = (P("seq", None), P(None, None, "bkt"), P("seq", "bkt"), P(None, "bkt", "seq"))
    out_specs = P(("seq", "bkt"), None)
    return jax.shard_map(
        per_device, mesh=mesh, in_specs=in_specs, out_specs=out_specs, check_vma=False
    )
```

```python
import functools
import math

import jax
import jax.numpy as jnp
from jax import lax
from jax.experimental import pallas as pl
from jax.experimental.pallas import tpu as pltpu
from jax.sharding import PartitionSpec as P

HH = 4
RR = 2
TT = 256
HS = 128
NO = 32
CAP = 12
ROWS = NO * 24
SLOTS = NO * CAP
MAIN = NO * 8
ITEMS = HH * RR
SCALE = 1.0 / math.sqrt(HS)
POWER = SCALE / math.log(2.0)
SELF_SCORE = -100000.0
FAR = -(2.0**30)
LSE_SHIFT = 4.5
F32 = jnp.float32
BF = jnp.bfloat16
VMEM = 24 * 1024 * 1024


def iota(shape, axis):
    return lax.broadcasted_iota(jnp.int32, shape, axis)


def dot(a, b, ca=1, cb=0, precision=None):
    return lax.dot_general(
        a, b, (((ca,), (cb,)), ((), ())), preferred_element_type=F32, precision=precision
    )


def halves(x):
    high = x.astype(BF)
    return high, (x - high.astype(F32)).astype(BF)


WIRE = HH * 3 * HS + 128
OWNERS = 32
PLACES = 40
CODES = 64


def dispatch_kernel(odd_ref, buckets_ref, proj_ref, cot_ref, rows_ref, out_ref):
    odd = odd_ref[0]
    before = (iota((TT, TT), 0) < iota((TT, TT), 1)).astype(BF)
    owner_ids = iota((NO, TT), 0)
    row_ids = iota((ROWS, TT), 0)
    buckets = [buckets_ref[r, h : h + 1, :] for r in range(RR) for h in range(HH)]
    hots = [owner_ids == lax.shift_right_logical(mine, 1) for mine in buckets]
    counts = dot(jnp.concatenate([hot.astype(BF) for hot in hots], axis=0), before)
    rows, ranks = [], []
    for item in range(ITEMS):
        count = counts[item * NO : (item + 1) * NO]
        rank = jnp.sum(jnp.where(hots[item], count, 0.0), axis=0, keepdims=True)
        rank = rank.astype(jnp.int32)
        first = item // HH
        late = 4 * odd if first == 0 else 4 - 4 * odd
        row = jnp.where(rank < 8, rank + 16 * first, rank + late)
        rows.append(lax.shift_right_logical(buckets[item], 1) * 24 + row)
        ranks.append(rank)
        rows_ref[item : item + 1, :] = rows[item]
    code_ids = iota((128, TT), 0)
    marks = jnp.zeros((ROWS, 128), F32)
    for h in range(HH):
        hot = ((row_ids == rows[h]) | (row_ids == rows[HH + h])).astype(BF)
        codes = 0
        for item, other in ((h, HH + h), (HH + h, h)):
            bucket = 1 + (buckets[item] & 1)
            codes = jnp.where((code_ids >= CODES) & (code_ids & 7 == item), bucket, codes)
            owner = lax.shift_right_logical(buckets[other], 1)
            codes = jnp.where(code_ids == OWNERS + item, owner, codes)
            codes = jnp.where(code_ids == PLACES + item, ranks[other], codes)
        codes = codes.astype(F32).astype(BF)
        lanes = pl.ds(h * HS, HS)
        source = jnp.concatenate(
            [proj_ref[0, :, lanes], proj_ref[1, :, lanes], cot_ref[:, lanes]], axis=1
        )
        out_ref[:, pl.ds(h * 3 * HS, 3 * HS)] = dot(hot, source).astype(BF)
        marks += dot(hot, codes, 1, 1)
    out_ref[:, pl.ds(HH * 3 * HS, 128)] = marks.astype(BF)


def dispatch(odd, buckets, proj, cot):
    vmem = pl.BlockSpec(memory_space=pltpu.VMEM)
    return pl.pallas_call(
        dispatch_kernel,
        out_shape=(
            jax.ShapeDtypeStruct((ITEMS, TT), jnp.int32),
            jax.ShapeDtypeStruct((ROWS, WIRE), BF),
        ),
        in_specs=[pl.BlockSpec(memory_space=pltpu.SMEM), vmem, vmem, vmem],
        compiler_params=pltpu.CompilerParams(vmem_limit_bytes=VMEM),
        name="dispatch",
    )(odd, buckets, proj, cot)


def split_rounds(x):
    width = x.shape[1]
    x = x.reshape(NO, 3, 8, width)
    mixed = x[:, 1].reshape(NO // 2, 2, 8, width)
    even, odd = mixed[:, 0], mixed[:, 1]
    top = iota((NO // 2, 8, width), 1) < 4
    late0 = jnp.where(top, even, odd).reshape(SLOTS - MAIN, width)
    late1 = jnp.where(top, odd, even).reshape(SLOTS - MAIN, width)
    return (
        jnp.concatenate([x[:, 0].reshape(MAIN, width), late0], axis=0),
        jnp.concatenate([x[:, 2].reshape(MAIN, width), late1], axis=0),
    )


def join_rounds(x0, x1):
    width = x0.shape[1]
    late0 = x0[MAIN:].reshape(NO // 2, 8, width)
    late1 = x1[MAIN:].reshape(NO // 2, 8, width)
    top = iota((NO // 2, 8, width), 1) < 4
    even = jnp.where(top, late0, late1)
    odd = jnp.where(top, late1, late0)
    mixed = jnp.stack([even, odd], axis=1).reshape(NO, 1, 8, width)
    main0 = x0[:MAIN].reshape(NO, 1, 8, width)
    main1 = x1[:MAIN].reshape(NO, 1, 8, width)
    return jnp.concatenate([main0, mixed, main1], axis=1).reshape(ROWS, width)


def source_and_slot(shape, axis, which):
    row = iota(shape, axis)
    late = row - MAIN
    flip = ((late & 7) >= 4).astype(jnp.int32)
    source_late = 2 * lax.shift_right_arithmetic(late, 3) + (flip if which == 0 else 1 - flip)
    source = jnp.where(row < MAIN, lax.shift_right_logical(row, 3), source_late)
    slot = jnp.where(row < MAIN, row & 7, 8 + (late & 3))
    return source, slot


def forward_kernel(
    x_ref,
    probs_ref,
    rows_ref,
    self_ref,
    wire_ref,
    mine_ref,
    probs,
    rows,
    kept_all,
    wire,
    mine,
    bias,
    spread,
    far,
    sems,
):
    lane = iota((SLOTS, HS), 1)
    for r in range(RR):
        source_i, slot_i = source_and_slot((SLOTS, 1), 0, r)
        source_j, slot_j = source_and_slot((1, SLOTS), 1, r)
        earlier = source_j * CAP + slot_j < source_i * CAP + slot_i
        bias[r] = jnp.where(earlier, 0.0, FAR)
    for r, marks in enumerate(split_rounds(x_ref[:, pl.ds(3 * HH * HS, HS)].astype(F32))):
        held = (lane >= OWNERS) & (lane < CODES) & ((lane & 7) >> 2 == r)
        spread[r] = jnp.where(held, marks, 0.0)
        group = lane & (HS - 8)
        wanted = jnp.where(group == CODES, 1.0, jnp.where(group == CODES + 8, 2.0, 0.0))
        coded = (group >= CODES) & (group < CODES + 24)
        far[r, :, :HS] = jnp.where(coded & (marks == wanted), FAR, 0.0).astype(BF)
        other = coded & ((marks != wanted) | (group == CODES + 16))
        far[r, :, HS:] = jnp.where(other, 1.0, 0.0).astype(BF)

    copies = []

    def send(here, there):
        copies.append(pltpu.make_async_copy(here, there, sems.at[len(copies)]))
        copies[-1].start()

    for h in range(HH):
        rounds = split_rounds(x_ref[:, pl.ds(h * 3 * HS, 3 * HS)].astype(F32))
        for r in range(RR):
            x = rounds[r].astype(BF)
            rows[h, r] = x
            send(rows.at[h, r], rows_ref.at[h, r])
            q = rounds[r][:, :HS]
            u = rounds[r][:, 2 * HS :]
            v_half = x[:, HS : 2 * HS]
            scale = lax.rsqrt(jnp.sum(q * q, axis=1, keepdims=True) + 1e-06)
            unit = (q * scale).astype(BF)
            far_q = far[r, :, :HS] * ((lane & 7) == r * HH + h).astype(BF)
            far_k = far[r, :, HS:]
            scores = dot(
                jnp.concatenate([x[:, :HS], far_q], axis=1),
                jnp.concatenate([unit, far_k], axis=1),
                1,
                1,
            )
            scores = scores + bias[r]
            top = jnp.maximum(jnp.max(scores, axis=1, keepdims=True), SELF_SCORE / SCALE)
            shifted = jnp.exp2((scores - top) * POWER).astype(BF)
            probs[h, r] = shifted
            send(probs.at[h, r], probs_ref.at[h, r])
            own = jnp.exp2((SELF_SCORE / SCALE - top) * POWER)
            both = dot(shifted, jnp.concatenate([v_half, jnp.ones_like(v_half)], axis=1))
            totals = both[:, HS:] + own
            inverse = 1.0 / totals
            own = (own * inverse).astype(BF).astype(F32)
            out = both[:, :HS] * inverse + own * rounds[r][:, HS : 2 * HS]
            out = out.astype(BF).astype(F32)
            inner = jnp.sum(u * out, axis=1, keepdims=True)
            lse = top * SCALE + jnp.log(totals)
            kept = 0.0
            for at, column in enumerate((own, inner, scale, inverse)):
                kept = jnp.where(lane == at, column.astype(F32), kept)
            kept_all[h, r] = kept
            send(kept_all.at[h, r], self_ref.at[h, r])
            at = lane - (r * HH + h) * 2
            sent = jnp.where(at == 0, lse - LSE_SHIFT, spread[r])
            spread[r] = jnp.where(at == 1, inner, sent)

    total = jnp.zeros((HS, SLOTS), F32)
    for r in range(RR):
        source, slot = source_and_slot((SLOTS, 1), 0, r)
        hot = (iota((SLOTS, SLOTS), 1) == slot * NO + source).astype(BF)
        total += dot(spread[r].astype(BF), hot, 0, 0)
    total = total.astype(BF)
    mine[...] = total
    total = total[: 2 * ITEMS]
    for k in range(NO):
        wire[pl.ds(k * 2 * ITEMS, 2 * ITEMS), :] = total
    quarter = NO * 2 * ITEMS // 4
    for at in range(4):
        part = pl.ds(at * quarter, quarter)
        send(wire.at[part], wire_ref.at[part])
    send(mine, mine_ref)
    for copy in copies:
        copy.wait()


def forward(received):
    shapes = (
        ((HH, RR, SLOTS, SLOTS), BF),
        ((HH, RR, SLOTS, 3 * HS), BF),
        ((HH, RR, SLOTS, HS), F32),
        ((NO * 2 * ITEMS, SLOTS), BF),
        ((HS, SLOTS), BF),
    )
    return pl.pallas_call(
        forward_kernel,
        out_shape=tuple(pltpu.HBM(*shape) for shape in shapes),
        in_specs=[pl.BlockSpec(memory_space=pltpu.VMEM)],
        out_specs=(pl.BlockSpec(memory_space=pl.ANY),) * len(shapes),
        scratch_shapes=[pltpu.VMEM(*shape) for shape in shapes]
        + [
            pltpu.VMEM((RR, SLOTS, SLOTS), F32),
            pltpu.VMEM((RR, SLOTS, HS), F32),
            pltpu.VMEM((RR, SLOTS, 2 * HS), BF),
            pltpu.SemaphoreType.DMA((3 * ITEMS + 5,)),
        ],
        compiler_params=pltpu.CompilerParams(vmem_limit_bytes=VMEM),
        name="forward",
    )(received)


def between_kernel(probs_ref, rows_ref, self_ref, probs_t_ref, weighted_t_ref, sums_ref):
    for r in range(RR):
        probs = (probs_ref[0, r].astype(F32) * self_ref[0, r, :, 3:4]).astype(BF)
        q = rows_ref[0, r, :, :HS]
        v = rows_ref[0, r, :, HS : 2 * HS]
        u = rows_ref[0, r, :, 2 * HS :]
        inner = self_ref[0, r, :, 1:2]
        scale = self_ref[0, r, :, 2:3]
        unit = (q.astype(F32) * scale).astype(BF)
        weighted = (probs.astype(F32) * (dot(u, v, 1, 1) - inner)).astype(BF)
        probs_t_ref[0, r] = probs.T
        weighted_t_ref[0, r] = weighted.T
        sums_ref[0, r, :, :HS] = dot(weighted, unit).astype(BF)
        sums_ref[0, r, :, HS : 2 * HS] = dot(probs, unit).astype(BF)
        own = self_ref[0, r, :, 0:1]
        sums_ref[0, r, :, 2 * HS :] = jnp.broadcast_to(own, (SLOTS, HS)).astype(BF)


SQUARE = pl.BlockSpec((1, RR, SLOTS, SLOTS), lambda h: (h, 0, 0, 0))
NARROW = pl.BlockSpec((1, RR, SLOTS, HS), lambda h: (h, 0, 0, 0))
WIDE = pl.BlockSpec((1, RR, SLOTS, 3 * HS), lambda h: (h, 0, 0, 0))


def between(probs, rows, own):
    flops = ITEMS * SLOTS * SLOTS * HS * 6
    return pl.pallas_call(
        between_kernel,
        grid=(HH,),
        out_shape=(
            pltpu.HBM((HH, RR, SLOTS, SLOTS), BF),
            pltpu.HBM((HH, RR, SLOTS, SLOTS), BF),
            pltpu.HBM((HH, RR, SLOTS, 3 * HS), BF),
        ),
        in_specs=[SQUARE, WIDE, NARROW],
        out_specs=(SQUARE, SQUARE, WIDE),
        compiler_params=pltpu.CompilerParams(vmem_limit_bytes=VMEM),
        cost_estimate=pl.CostEstimate(flops=flops, bytes_accessed=12 << 20, transcendentals=0),
        name="between",
    )(pinned(probs), pinned(rows), pinned(own))


def round_shares(mine_ref, got_ref, got, put):
    for at in range(SLOTS // HS):
        got[at, : NO * 2 * ITEMS] = got_ref[:, pl.ds(at * HS, HS)].astype(F32)
    mine = mine_ref[...].astype(F32)
    owner_ids = iota((3 * NO, SLOTS), 0)
    slot_ids = iota((HS, SLOTS), 0)
    source = iota((1, SLOTS), 1) & (NO - 1)
    mine_lse, mine_inner, other_lse, other_inner = [], [], [], []
    for item in range(ITEMS):
        first_row = (item ^ HH) * 2
        table = jnp.concatenate(
            [
                jnp.concatenate(
                    [
                        got[i, pl.ds(first_row + at, NO, stride=2 * ITEMS), :]
                        for i in range(SLOTS // HS)
                    ],
                    axis=0,
                ).astype(BF)
                for at in range(2)
            ],
            axis=1,
        )
        owner = mine[OWNERS + item : OWNERS + item + 1].astype(jnp.int32)
        slot = mine[PLACES + item : PLACES + item + 1].astype(jnp.int32)
        hot = (owner_ids == lax.shift_right_logical(slot, 2) * NO + owner).astype(BF)
        here = slot_ids == (slot & 3) * NO + source
        seen = dot(table, hot, 0, 0)
        other_lse.append(jnp.sum(jnp.where(here, seen[:HS], 0.0), axis=0, keepdims=True))
        other_inner.append(jnp.sum(jnp.where(here, seen[HS:], 0.0), axis=0, keepdims=True))
        mine_lse.append(mine[item * 2 : item * 2 + 1])
        mine_inner.append(mine[item * 2 + 1 : item * 2 + 2])
    mine_lse, mine_inner, other_lse, other_inner = (
        jnp.concatenate(x, axis=0) for x in (mine_lse, mine_inner, other_lse, other_inner)
    )
    top = jnp.maximum(mine_lse, other_lse)
    share = jnp.exp(mine_lse - top)
    other_share = jnp.exp(other_lse - top)
    inverse = 1.0 / (share + other_share)
    share = share * inverse
    shift = other_share * inverse * (other_inner - mine_inner)
    high, low = halves(jnp.concatenate([share, shift], axis=0))
    both = jnp.concatenate([high, low], axis=1)
    for r in range(RR):
        source, slot = source_and_slot((SLOTS, 1), 0, r)
        hot = (iota((SLOTS, SLOTS), 1) == slot * NO + source).astype(BF)
        columns = dot(jnp.concatenate([hot, hot], axis=1), both, 1, 1)
        for h in range(HH):
            item = r * HH + h
            put[h, r, :, :HS] = jnp.broadcast_to(columns[:, item : item + 1], (SLOTS, HS))
            item += ITEMS
            put[h, r, :, HS:] = jnp.broadcast_to(columns[:, item : item + 1], (SLOTS, HS))


def backward_kernel(
    probs_ref,
    weighted_ref,
    rows_ref,
    sums_ref,
    mine_ref,
    got_ref,
    out_ref,
    probs,
    weighted,
    queries,
    upstream,
    sums,
    out,
    got,
    put,
    sems,
):
    loads = []
    for h in range(HH):
        pairs = (
            (probs_ref.at[h], probs.at[h]),
            (weighted_ref.at[h], weighted.at[h]),
            (rows_ref.at[h, :, :, pl.ds(0, HS)], queries.at[h]),
            (rows_ref.at[h, :, :, pl.ds(2 * HS, HS)], upstream.at[h]),
            (sums_ref.at[h], sums.at[h]),
        )
        loads.append(
            [pltpu.make_async_copy(*p, sems.at[5 * h + at]) for at, p in enumerate(pairs)]
        )
        for copy in loads[h]:
            copy.start()
    round_shares(mine_ref, got_ref, got, put)
    stores = []
    for h in range(HH):
        for copy in loads[h]:
            copy.wait()
        grads = []
        for r in range(RR):
            share = put[h, r, :, :HS]
            shift = put[h, r, :, HS:]
            q = queries[h, r].astype(F32)
            u_share = share * upstream[h, r].astype(F32)
            q_share = share * q
            right = jnp.concatenate([-shift * q_share, u_share], axis=1).astype(BF)
            both = dot(probs[h, r], right)
            unit_grad = (dot(weighted[h, r], q_share.astype(BF)) + both[:, :HS]) * SCALE
            value_grad = both[:, HS:] + sums[h, r, :, 2 * HS :].astype(F32) * u_share
            scale = lax.rsqrt(jnp.sum(q * q, axis=1, keepdims=True) + 1e-06)
            along = jnp.sum(q * unit_grad, axis=1, keepdims=True)
            first = sums[h, r, :, :HS].astype(F32)
            second = sums[h, r, :, HS : 2 * HS].astype(F32)
            query_grad = (share * SCALE) * (first - shift * second)
            query_grad += scale * unit_grad - q * (scale * scale * scale * along)
            grads.append(jnp.concatenate([query_grad, value_grad], axis=1))
        out[h] = join_rounds(grads[0], grads[1]).astype(BF)
        for at in range(2):
            part = pl.ds(at * (ROWS // 2), ROWS // 2)
            there = out_ref.at[part, pl.ds(h * 2 * HS, 2 * HS)]
            sem = sems.at[5 * HH + 2 * h + at]
            stores.append(pltpu.make_async_copy(out.at[h, part], there, sem))
            stores[-1].start()
    for copy in stores:
        copy.wait()


def pinned(x):
    return pltpu.with_memory_space_constraint(x, pltpu.HBM)


def backward(probs, weighted, rows, sums, mine, got):
    hbm = pl.BlockSpec(memory_space=pl.ANY)
    vmem = pl.BlockSpec(memory_space=pltpu.VMEM)
    return pl.pallas_call(
        backward_kernel,
        out_shape=pltpu.HBM((ROWS, HH * 2 * HS), BF),
        in_specs=[hbm, hbm, hbm, hbm, vmem, vmem],
        out_specs=hbm,
        scratch_shapes=[
            pltpu.VMEM((HH, RR, SLOTS, SLOTS), BF),
            pltpu.VMEM((HH, RR, SLOTS, SLOTS), BF),
            pltpu.VMEM((HH, RR, SLOTS, HS), BF),
            pltpu.VMEM((HH, RR, SLOTS, HS), BF),
            pltpu.VMEM((HH, RR, SLOTS, 3 * HS), BF),
            pltpu.VMEM((HH, ROWS, 2 * HS), BF),
            pltpu.VMEM((SLOTS // HS, (NO + 1) * 2 * ITEMS, HS), F32),
            pltpu.VMEM((HH, RR, SLOTS, 2 * HS), F32),
            pltpu.SemaphoreType.DMA((7 * HH,)),
        ],
        compiler_params=pltpu.CompilerParams(vmem_limit_bytes=VMEM),
        name="backward",
    )(pinned(probs), pinned(weighted), pinned(rows), pinned(sums), mine, got)


def collect_kernel(rows_ref, got_ref, out_ref):
    row_ids = iota((TT, ROWS), 1)
    for h in range(HH):
        first = row_ids == rows_ref[:, h : h + 1]
        second = row_ids == rows_ref[:, HH + h : HH + h + 1]
        hot = (first | second).astype(BF)
        sums = dot(hot, got_ref[:, pl.ds(h * 2 * HS, 2 * HS)]).astype(BF)
        out_ref[0, :, pl.ds(h * HS, HS)] = sums[:, :HS]
        out_ref[1, :, pl.ds(h * HS, HS)] = sums[:, HS:]


def collect(rows, got):
    vmem = pl.BlockSpec(memory_space=pltpu.VMEM)
    return pl.pallas_call(
        collect_kernel,
        out_shape=jax.ShapeDtypeStruct((2, TT, HH * HS), BF),
        in_specs=[vmem, vmem],
        out_specs=vmem,
        compiler_params=pltpu.CompilerParams(vmem_limit_bytes=12 * 1024 * 1024),
        name="collect",
    )(rows, got)


def exchange(x):
    return lax.all_to_all(x, "seq", split_axis=0, concat_axis=0, tiled=True)


def block_order(me):
    return [me, me ^ 3, me ^ 1, me ^ 2]


def blocks_of(x, me):
    size = x.shape[1] // 4
    parts = [lax.dynamic_slice_in_dim(x, i * size, size, 1) for i in block_order(me)]
    return jnp.concatenate(parts, axis=1)


def swap(x, mask):
    return lax.ppermute(x, "bkt", [(i, i ^ mask) for i in range(4)])


PARTS = 4


def per_device(tokens, weights, cotangent, buckets):
    odd = (lax.axis_index("seq") & 1).astype(jnp.int32).reshape(1)
    me = lax.axis_index("bkt")
    projected = jnp.einsum(
        "td,dcf->ctf", tokens, weights, preferred_element_type=jnp.float32
    ).astype(jnp.bfloat16)
    rows, send = dispatch(odd, buckets, projected, cotangent)
    received = exchange(send)
    rows = blocks_of(rows, me).T
    probs, held, own, wire, mine = forward(received)
    everyones = exchange(wire)
    probs_t, weighted_t, sums = between(probs, held, own)
    slot_grads = exchange(backward(probs_t, weighted_t, held, sums, mine, everyones))
    grads = collect(rows, slot_grads)
    width = weights.shape[0] // PARTS
    slabs = lax.optimization_barrier(
        [weights[i * width : (i + 1) * width].transpose(1, 0, 2) for i in range(PARTS)]
    )
    sums = []
    for i, slab in enumerate(slabs):
        part = jnp.einsum("ctf,cdf->td", grads, slab, preferred_element_type=jnp.float32)
        part = part.astype(jnp.bfloat16).reshape(4, TT // 4, width)
        if i % 2 == 0:
            sums.append(part[:2] + swap(part[2:], 1))
        else:
            sums.append(
                jnp.stack([part[0], part[2]]) + swap(jnp.stack([part[1], part[3]]), 3)
            )
    outs = [x[0] + swap(x[1], 3 if i % 2 == 0 else 1) for i, x in enumerate(sums)]
    return jnp.concatenate(outs, axis=1)


def solution(mesh):
    in_specs = (P("seq", None), P(None, None, "bkt"), P("seq", "bkt"), P(None, "bkt", "seq"))
    out_specs = P(("seq", "bkt"), None)
    return jax.shard_map(
        per_device, mesh=mesh, in_specs=in_specs, out_specs=out_specs, check_vma=False
    )
```
